512 devices in a mesh: row: 16 (over z), col: 32 (over y, x, core).
Axes of the slice: x: 4, y: 4, z: 16, core: 2. Of those that a mesh axis runs over, the one named last changes fastest.
Arguments:
- weight: bfloat16 [8192, 28672], P('row', 'col'), may hold values from -3 to 3
- gradient: bfloat16 [8192, 28672], P('row', 'col'), may hold values from -6 to 6
- momentum: bfloat16 [8192, 28672], P('row', 'col'), may hold values from -6 to 6
- basis: bfloat16 [28672, 512], P('col', 'row'), may hold values from -6 to 6
Outputs:
- new_weight: bfloat16 [8192, 28672], P('row', 'col')
- new_momentum: bfloat16 [8192, 28672], P('row', 'col')
- new_basis: bfloat16 [28672, 512], P('col', 'row')
The draws below stay inside these ranges and needn't reach their ends.
All inputs are finite; a program needn't handle non-finite values.
Results may differ from the reference program's by a relative error of at most 0.012.
Values may be sent and summed in bfloat16 or wider, within the bound.
A program may use at most 64 MiB of HBM per device.

```python
import math
import jax
import jax.numpy as jnp
from jax import lax

D = 8192
FF = 28672
RANK = 512


def shard_levels(rng, shape, cuts, low, high):
    factor_of, own = 1.0, jax.random.fold_in(rng, 6)
    for position, blocks in cuts:
        steps = jnp.exp(jax.random.uniform(jax.random.fold_in(own, position), (blocks,), jnp.float32, low / len(cuts), high / len(cuts)))
        factor_of = factor_of * jnp.repeat(steps, shape[position] // blocks).reshape([-1 if axis == position else 1 for axis in range(len(shape))])
    return factor_of


def centred(own_key, shape, scale, bound, split=(), held_as=jnp.bfloat16):
    gain = shard_levels(own_key, shape, split, -0.22, 0.18) if split else 1.0
    values = jax.random.normal(own_key, shape, jnp.float32) * scale * gain
    return jnp.minimum(jnp.maximum(values, -bound), bound).astype(held_as)


def setup_inputs(seed: int = 0) -> dict:
    key_of = jax.random.split(jax.random.key(seed), 5)
    return {
        "weight": centred(key_of[0], (D, FF), 0.5, 3.0, ((0, 16), (1, 32))),
        "gradient": centred(key_of[1], (D, FF), 1.0, 6.0, ((0, 16), (1, 32))),
        "momentum": centred(key_of[2], (D, FF), 1.0, 6.0, ((0, 16), (1, 32))),
        "basis": centred(key_of[3], (FF, RANK), 1.0, 6.0, ((0, 32), (1, 16))),
    }


def solve_right(factor, values):
    return lax.linalg.triangular_solve(factor, values, left_side=False, lower=True, transpose_a=True)

def reference(weight, gradient, momentum, basis):
    buffer = (momentum.astype(jnp.float32) + gradient.astype(jnp.float32)).astype(jnp.bfloat16)
    left = jnp.dot(buffer.astype(jnp.float32), basis.astype(jnp.float32), preferred_element_type=jnp.float32).astype(jnp.bfloat16)
    gram = jnp.dot(left.T.astype(jnp.float32), left.astype(jnp.float32), preferred_element_type=jnp.float32)
    factor = jnp.linalg.cholesky(gram)
    ortho = solve_right(factor, left.astype(jnp.float32))
    cross = jnp.dot(buffer.T.astype(jnp.float32), left.astype(jnp.float32), preferred_element_type=jnp.float32)
    right = solve_right(factor, cross)
    scale = lax.rsqrt(lax.optimization_barrier(jnp.mean(right * right, axis=0)) + 1e-06)
    new_basis = (right * scale[None, :]).astype(jnp.bfloat16)
    correction = jnp.dot(ortho, right.T, precision=lax.Precision.HIGHEST)
    new_momentum = (buffer.astype(jnp.float32) - 0.2 * correction).astype(jnp.bfloat16)
    update = jnp.dot(ortho.astype(jnp.bfloat16).astype(jnp.float32), new_basis.T.astype(jnp.float32), preferred_element_type=jnp.float32)
    new_weight = (weight.astype(jnp.float32) - 0.5 * math.sqrt(D / RANK) * update).astype(jnp.bfloat16)
    return (new_weight, new_momentum, new_basis)
```

```python
import math

import jax
import jax.numpy as jnp
from jax import lax
from jax.experimental import pallas as pl
from jax.experimental.pallas import tpu as pltpu
from jax.sharding import PartitionSpec as P

D = 8192
FF = 28672
RANK = 512
ROWS = 16
COLS = 32
TILES = 5
F32 = jnp.float32
BF16 = jnp.bfloat16
HIGHEST = lax.Precision.HIGHEST
MESH = pl.DeviceIdType.MESH
VMEM = pl.BlockSpec(memory_space=pltpu.VMEM)
ANY = pl.BlockSpec(memory_space=pl.ANY)
DMA = pltpu.SemaphoreType.DMA
NN = (((1,), (0,)), ((), ()))
NT = (((1,), (1,)), ((), ()))
TN = (((0,), (0,)), ((), ()))


def remote(src, dst, send, recv, **where):
    return pltpu.make_async_remote_copy(
        src_ref=src, dst_ref=dst, send_sem=send, recv_sem=recv, device_id=where, device_id_type=MESH)


def wait_bytes(ref, sem):
    pltpu.make_async_copy(ref, ref, sem).wait()


def ring(a):
    return lax.rem(a + 2 * ROWS, ROWS)


def greet(r, c):
    barrier = pltpu.get_barrier_semaphore()
    for k in (1, 2, ROWS - 1, ROWS - 2):
        pl.semaphore_signal(barrier, inc=1, device_id={"row": ring(r + k)}, device_id_type=MESH)

    def one(k, carry):
        pl.semaphore_signal(barrier, inc=1, device_id={"col": lax.rem(c + k, COLS)}, device_id_type=MESH)
        return carry

    lax.fori_loop(1, COLS, one, 0)
    return barrier, 4 + COLS - 1


def col_send(c, src_of, dst, send, recv):
    def one(k, carry):
        d = lax.rem(c + k, COLS)
        remote(src_of(d), dst, send, recv, col=d).start()
        return carry

    lax.fori_loop(1, COLS, one, 0)


class Gather:
    def __init__(self, r, buf, send, recv):
        self.r, self.buf, self.send, self.recv = r, buf, send, recv

    def message(self, way, d):
        sign = 1 if way == 0 else -1
        step = jnp.minimum(d, 2)
        block = self.buf.at[ring(self.r - sign * (d - step))]
        return remote(block, block, self.send.at[way, d], self.recv.at[way, d], row=ring(self.r + sign * step))

    def start(self):
        for d in (2, 1):
            for way in range(2):
                self.message(way, d).start()

    def forward(self, d):
        for way in range(2):
            self.message(way, d).wait_recv()
            last = 8 - way

            @pl.when(d + 2 <= last)
            def _():
                self.message(way, d + 2).start()

    def end(self, d):
        self.message(0, d).wait_recv()

        @pl.when(d <= 7)
        def _():
            self.message(1, d).wait_recv()

    def drain(self):
        def one(d, carry):
            self.message(0, d).wait_send()

            @pl.when(d <= 7)
            def _():
                self.message(1, d).wait_send()

            return carry

        lax.fori_loop(1, 9, one, 0)


class Reduce:
    def __init__(self, r, part, slots, first, send, recv):
        self.r, self.part, self.slots, self.first, self.send, self.recv = r, part, slots, first, send, recv
        self.size = RANK // ROWS

    def own(self, block):
        return self.part[pl.ds(pl.multiple_of(block * self.size, self.size), self.size), :]

    def message(self, way, d, src):
        sign = 1 if way == 0 else -1
        return remote(
            src, self.slots.at[way, d], self.send.at[way, d], self.recv.at[way, d],
            row=ring(self.r + sign * jnp.minimum(d, 2)))

    def start(self):
        for i in range(2):
            for way in range(2):
                d = 8 - way - i
                here = self.first.at[way, i]
                here[...] = self.own(ring(self.r + (d if way == 0 else -d))).astype(BF16)
                self.message(way, d, here).start()

    def forward(self, k):
        for way in range(2):
            def go():
                d = 6 - way - k
                got = self.slots.at[way, d + 2]
                self.message(way, d + 2, got).wait_recv()
                got[...] = (got[...].astype(F32) + self.own(ring(self.r + (d if way == 0 else -d)))).astype(BF16)
                self.message(way, d, got).start()

            if way == 0:
                go()
            else:
                pl.when(k < 5)(go)

    def end(self):
        total = self.own(self.r)
        for way in range(2):
            for d in (2, 1):
                self.message(way, d, self.first.at[0, 0]).wait_recv()
                total = total + self.slots[way, d].astype(F32)
        return total

    def drain(self):
        def one(d, carry):
            self.message(0, d, self.first.at[0, 0]).wait_send()

            @pl.when(d <= 7)
            def _():
                self.message(1, d, self.first.at[0, 0]).wait_send()

            return carry

        lax.fori_loop(1, 9, one, 0)


def split(x):
    high = x.astype(BF16)
    return high, (x - high.astype(F32)).astype(BF16)


def factor_block(w):
    sub = lax.broadcasted_iota(jnp.int32, (8, 256), 0)

    def twice(x):
        return jnp.concatenate([x, x], axis=1)

    for p in range(16):
        panel = w[p]
        columns = [jnp.broadcast_to(panel[:, 8 * p + j:8 * p + j + 1], (8, 128)) for j in range(8)]
        s = {}
        for j in range(8):
            for i in range(j + 1):
                s[i, j] = jnp.broadcast_to(columns[j][i:i + 1, :], (8, 128))
        rows = [jnp.broadcast_to(panel[k:k + 1, :], (8, 256)) for k in range(8)]
        for j in range(8):
            root = lax.rsqrt(s[j, j])
            u = {i: s[j, i] * root for i in range(j + 1, 8)}
            for i in range(j + 1, 8):
                for l in range(i, 8):
                    s[i, l] = s[i, l] - u[i] * u[l]
            rows[j] = rows[j] * twice(root)
            for i in range(j + 1, 8):
                rows[i] = rows[i] - twice(u[i]) * rows[j]
        done = rows[7]
        for k in range(7):
            done = jnp.where(sub == k, rows[k], done)
        w[p] = done
        if p < 15:
            turned = done[:, :128].T
            for g in range(p + 1, 16):
                rest = w[g]
                for k in range(8):
                    rest = rest - jnp.broadcast_to(turned[8 * g:8 * g + 8, k:k + 1], (8, 256)) * rows[k]
                w[g] = rest


def unit(rows):
    return jnp.where(
        lax.broadcasted_iota(jnp.int32, (rows, rows), 0) == lax.broadcasted_iota(jnp.int32, (rows, rows), 1), 1.0, 0.0)


def main_kernel(
    basis_in, momentum, gradient, ortho_out, right_out, sums_out,
    basis_all, loaded, buffer, partial, arrived, lefts, left, order, cross_part, slots, first, cross_all,
    gram_part, gram_send, gram_recv, gram_tiles, gram_all, work, block, sums,
    load_sems, basis_send, basis_recv, red_send, red_recv, cross_send, cross_recv, left_sems, sems,
):
    r, c = lax.axis_index("row"), lax.axis_index("col")
    core = lax.rem(c, 2)
    barrier, count = greet(r, c)
    loads = [
        pltpu.make_async_copy(basis_in, basis_all.at[r], load_sems.at[0]),
        pltpu.make_async_copy(momentum, loaded.at[0], load_sems.at[1]),
        pltpu.make_async_copy(gradient, loaded.at[1], load_sems.at[2]),
    ]
    for load in loads:
        load.start()
    work[:, 512:] = jnp.zeros((512, 512), F32)
    for b in range(4):
        work[128 * b:128 * b + 128, 512 + 128 * b:512 + 128 * b + 128] = unit(128)
    place = lax.broadcasted_iota(jnp.int32, (512, 512), 0)
    turn = (place >> 5) & 3
    far = 2 * (place >> 7) + 1 + (turn >> 1)
    source = jnp.where(place >= 480, r, jnp.where((turn & 1) == 0, r - far, r + far)) & (ROWS - 1)
    natural = source * 32 + (place & 31)
    order[...] = jnp.where(natural == lax.broadcasted_iota(jnp.int32, (512, 512), 1), 1.0, 0.0).astype(BF16)
    for load in loads:
        load.wait()
    buffer[...] = (loaded[0].astype(F32) + loaded[1].astype(F32)).astype(BF16)
    pl.semaphore_wait(barrier, count)

    gather = Gather(r, basis_all, basis_send, basis_recv)
    gather.start()

    def send_partial(w):
        if w < 3:
            for d in (2 * w + 1, 2 * w + 2):
                gather.forward(d)
            ids = [r - (2 * w + 1), r + (2 * w + 1), r - (2 * w + 2), r + (2 * w + 2)]
        else:
            gather.end(7)
            gather.end(8)
            ids = [r - 7, r + 7, r - 8, r]
        columns = jnp.concatenate([basis_all[ring(i)] for i in ids], axis=0)
        partial[w] = lax.dot_general(buffer[...], columns, NT, preferred_element_type=F32).astype(BF16)

        def rows_of(d):
            return partial.at[w, pl.ds(pl.multiple_of(d * 16, 16), 16), :]

        col_send(c, rows_of, arrived.at[w, c], left_sems.at[0, w], left_sems.at[1, w])
        arrived[w, c] = rows_of(c)[...]

    def send_left(w):
        wait_bytes(arrived.at[w, pl.ds(0, COLS - 1)], left_sems.at[1, w])
        total = arrived[w, 0].astype(F32)
        for k in range(1, COLS):
            total = total + arrived[w, k].astype(F32)
        lefts[w, c] = total.astype(BF16)
        col_send(c, lambda d: lefts.at[w, c], lefts.at[w, c], left_sems.at[2, w], left_sems.at[3, w])

    for w in range(4):
        send_partial(w)
        if w > 0:
            send_left(w - 1)
    send_left(3)
    for w in range(4):
        wait_bytes(arrived.at[w, pl.ds(0, COLS - 1)], left_sems.at[3, w])
    mixed = jnp.concatenate([lefts[w].reshape(512, 128) for w in range(4)], axis=1)
    left[...] = jnp.dot(mixed, order[...], preferred_element_type=F32).astype(BF16)

    quarter = c // 16
    for i in range(2):
        start = quarter if i == 0 else 3 - quarter
        lanes = left[:, pl.ds(pl.multiple_of(start * 128, 128), 128)]
        gram_part[i] = lax.dot_general(lanes, left[...], TN, preferred_element_type=F32)
    low = lax.rem(c, 16)
    for t in range(TILES):
        upper = t < 4 - quarter
        part = jnp.where(upper, 0, 1)
        row = jnp.where(upper, low, 15 - low)
        lane = jnp.where(upper, t + quarter, t - 1)
        gram_send[t] = gram_part[part, pl.ds(pl.multiple_of(row * 8, 8), 8), pl.ds(pl.multiple_of(lane * 128, 128), 128)]

    mine = lax.rem(r, 8)
    reducer = mine < TILES

    def send_tile(k, carry):
        d = ring(r + k)
        t = lax.rem(d, 8)

        @pl.when(t < TILES)
        def _():
            remote(gram_send.at[t], gram_recv.at[r], sems.at[0], sems.at[1], row=d).start()

        return carry

    lax.fori_loop(1, ROWS, send_tile, 0)

    for n in range(2):
        cross_part[256 * n:256 * n + 256, :] = lax.dot_general(
            left[:, 256 * n:256 * n + 256], buffer[...], TN, preferred_element_type=F32)
    reduce = Reduce(r, cross_part, slots, first, red_send, red_recv)
    reduce.start()

    @pl.when(reducer)
    def _():
        wait_bytes(gram_recv.at[pl.ds(0, ROWS - 1)], sems.at[1])
        gram_recv[r] = gram_send[mine]
        tile = gram_recv[0]
        for k in range(1, ROWS):
            tile = tile + gram_recv[k]
        gram_tiles[mine] = tile
        for k in (-3, -2, -1, 1, 2, 3, 4):
            remote(gram_tiles.at[mine], gram_tiles.at[mine], sems.at[2], sems.at[3], row=ring(r + k)).start()

    for k in range(2):
        reduce.forward(k)

    @pl.when(reducer)
    def _():
        wait_bytes(gram_recv.at[pl.ds(0, TILES - 1)], sems.at[3])

    @pl.when(jnp.logical_not(reducer))
    def _():
        wait_bytes(gram_recv.at[pl.ds(0, TILES)], sems.at[3])

    chip = c // 2
    gram_all[core, chip] = gram_tiles[...]

    def send_gram(k, carry):
        remote(gram_all.at[core, chip], gram_all.at[core, chip], sems.at[4], sems.at[5],
               col=lax.rem(c + 2 * k, COLS)).start()
        return carry

    lax.fori_loop(1, COLS // 2, send_gram, 0)
    for k in range(2, 4):
        reduce.forward(k)
    wait_bytes(gram_all.at[0, pl.ds(0, 15)], sems.at[5])
    sibling = remote(gram_all.at[core], gram_all.at[core], sems.at[6], sems.at[7], col=c + 1 - 2 * core)
    sibling.start()
    for k in range(4, 6):
        reduce.forward(k)
    sibling.wait_recv()

    def place_tiles(k, carry):
        kc = 2 * (k // 2) + lax.rem(k, 2)
        kq = kc // 16
        for t in range(TILES):
            upper = t < 4 - kq
            row = jnp.where(upper, kc, 63 - kc)
            lane = jnp.where(upper, t + kq, t - 1)
            work[pl.ds(pl.multiple_of(row * 8, 8), 8), pl.ds(pl.multiple_of(lane * 128, 128), 128)] = (
                gram_all[lax.rem(k, 2), k // 2, t])
        return carry

    lax.fori_loop(0, COLS, place_tiles, 0)
    cross_all[r] = reduce.end().astype(BF16)
    spread = Gather(r, cross_all, cross_send, cross_recv)
    spread.start()

    def factor_step(b, carry):
        rows = pl.ds(pl.multiple_of(128 * b, 128), 128)
        live = pl.ds(pl.multiple_of(128 * (b + 1), 128), 512)
        block[:, :, :128] = work[rows, rows].reshape(16, 8, 128)
        block[:, :, 128:] = unit(128).reshape(16, 8, 128)
        factor_block(block)
        inverse = block[:, :, 128:].reshape(128, 128)
        panel = lax.dot_general(inverse, work[rows, live], NN, precision=HIGHEST, preferred_element_type=F32)
        work[rows, live] = panel

        def trail(i, carry):
            lanes = pl.ds(pl.multiple_of(128 * i, 128), 128)
            work[lanes, live] = work[lanes, live] - lax.dot_general(
                work[rows, lanes], panel, TN, precision=HIGHEST, preferred_element_type=F32)
            return carry

        lax.fori_loop(b + 1, 4, trail, 0)

        @pl.when(b < 3)
        def _():
            spread.forward(2 * b + 1)
            spread.forward(2 * b + 2)

        return carry

    lax.fori_loop(0, 4, factor_step, 0)
    spread.end(7)
    spread.end(8)

    high, low_part = split(work[:, 512:])
    cross = cross_all[...].reshape(512, 896)
    right = jnp.dot(high, cross, preferred_element_type=F32) + jnp.dot(low_part, cross, preferred_element_type=F32)
    right_out[...] = right
    square_high, square_low = split(right * right)
    ones = jnp.ones((8, 896), BF16)
    total = (
        lax.dot_general(ones, square_high, NT, preferred_element_type=F32)
        + lax.dot_general(ones, square_low, NT, preferred_element_type=F32))
    sub = lax.broadcasted_iota(jnp.int32, (8, 128), 0)
    tile = total[:, :128]
    for q in range(1, 4):
        tile = jnp.where(sub == q, total[:, 128 * q:128 * q + 128], tile)
    sums[c] = tile
    col_send(c, lambda d: sums.at[c], sums.at[c], sems.at[8], sems.at[9])
    ortho_out[...] = (
        lax.dot_general(left[...], high, NT, preferred_element_type=F32)
        + lax.dot_general(left[...], low_part, NT, preferred_element_type=F32)).astype(BF16)

    gather.drain()
    reduce.drain()
    spread.drain()
    for w in range(4):
        wait_bytes(arrived.at[w, pl.ds(0, COLS - 1)], left_sems.at[0, w])
        wait_bytes(arrived.at[w, pl.ds(0, COLS - 1)], left_sems.at[2, w])

    @pl.when(reducer)
    def _():
        wait_bytes(gram_recv.at[pl.ds(0, 2 * TILES - 1)], sems.at[0])
        wait_bytes(gram_recv.at[pl.ds(0, 7)], sems.at[2])

    @pl.when(jnp.logical_not(reducer))
    def _():
        wait_bytes(gram_recv.at[pl.ds(0, 2 * TILES)], sems.at[0])

    wait_bytes(gram_all.at[0, pl.ds(0, 15)], sems.at[4])
    sibling.wait_send()
    wait_bytes(sums.at[pl.ds(0, COLS - 1)], sems.at[8])
    wait_bytes(sums.at[pl.ds(0, COLS - 1)], sems.at[9])
    total = sums[0]
    for k in range(1, COLS):
        total = total + sums[k]
    sums_out[...] = total


def main_call(basis_t, momentum, gradient):
    return pl.pallas_call(
        main_kernel,
        out_shape=[
            jax.ShapeDtypeStruct((512, 512), BF16),
            jax.ShapeDtypeStruct((512, 896), F32),
            jax.ShapeDtypeStruct((8, 128), F32),
        ],
        in_specs=[ANY] * 3,
        out_specs=[VMEM] * 3,
        scratch_shapes=[
            pltpu.VMEM((ROWS, 32, 896), BF16),
            pltpu.VMEM((2, 512, 896), BF16),
            pltpu.VMEM((512, 896), BF16),
            pltpu.VMEM((4, 512, 128), BF16),
            pltpu.VMEM((4, COLS, 16, 128), BF16),
            pltpu.VMEM((4, COLS, 16, 128), BF16),
            pltpu.VMEM((512, 512), BF16),
            pltpu.VMEM((512, 512), BF16),
            pltpu.VMEM((512, 896), F32),
            pltpu.VMEM((2, 9, 32, 896), BF16),
            pltpu.VMEM((2, 2, 32, 896), BF16),
            pltpu.VMEM((ROWS, 32, 896), BF16),
            pltpu.VMEM((2, 128, 512), F32),
            pltpu.VMEM((TILES, 8, 128), F32),
            pltpu.VMEM((ROWS, 8, 128), F32),
            pltpu.VMEM((TILES, 8, 128), F32),
            pltpu.VMEM((2, COLS // 2, TILES, 8, 128), F32),
            pltpu.VMEM((512, 1024), F32),
            pltpu.VMEM((16, 8, 256), F32),
            pltpu.VMEM((COLS, 8, 128), F32),
            DMA((3,)),
            DMA((2, 9)), DMA((2, 9)),
            DMA((2, 9)), DMA((2, 9)),
            DMA((2, 9)), DMA((2, 9)),
            DMA((4, 4)),
            DMA((10,)),
        ],
        compiler_params=pltpu.CompilerParams(
            collective_id=0, has_side_effects=True, vmem_limit_bytes=56 * 2**20),
    )(basis_t, momentum, gradient)


def out_kernel(ortho, right, sums, momentum, gradient, weight, new_weight, new_momentum, new_basis_t, values, basis, mine):
    @pl.when(pl.program_id(0) == 0)
    def _():
        scale = lax.rsqrt(sums[...] / FF + 1e-06).T
        for q in range(4):
            rows = slice(128 * q, 128 * q + 128)
            mine[rows, :] = right[rows, :] * scale[:, q:q + 1]
            values[rows, :] = right[rows, :].astype(BF16)
            basis[rows, :] = mine[rows, :].astype(BF16)
        r = lax.axis_index("row")
        new_basis_t[...] = mine[pl.ds(pl.multiple_of(r * 32, 32), 32), :].astype(BF16)

    correction = jnp.dot(ortho[...], values[...], preferred_element_type=F32)
    buffer = (momentum[...].astype(F32) + gradient[...].astype(F32)).astype(BF16).astype(F32)
    new_momentum[...] = (buffer - 0.2 * correction).astype(BF16)
    update = jnp.dot(ortho[...], basis[...], preferred_element_type=F32)
    new_weight[...] = (weight[...].astype(F32) - 0.5 * math.sqrt(D / RANK) * update).astype(BF16)


def out_call(ortho, right, sums, momentum, gradient, weight):
    slab = pl.BlockSpec((128, 896), lambda i: (i, 0))
    return pl.pallas_call(
        out_kernel,
        grid=(4,),
        out_shape=[
            jax.ShapeDtypeStruct((512, 896), BF16),
            jax.ShapeDtypeStruct((512, 896), BF16),
            jax.ShapeDtypeStruct((32, 896), BF16),
        ],
        in_specs=[
            pl.BlockSpec((128, 512), lambda i: (i, 0)),
            pl.BlockSpec((512, 896), lambda i: (0, 0)),
            pl.BlockSpec((8, 128), lambda i: (0, 0)),
            slab, slab, slab,
        ],
        out_specs=[slab, slab, pl.BlockSpec((32, 896), lambda i: (0, 0))],
        scratch_shapes=[
            pltpu.VMEM((512, 896), BF16),
            pltpu.VMEM((512, 896), BF16),
            pltpu.VMEM((512, 896), F32),
        ],
        compiler_params=pltpu.CompilerParams(vmem_limit_bytes=32 * 2**20),
    )(ortho, right, sums, momentum, gradient, weight)


def local(weight, gradient, momentum, basis):
    ortho, right, sums = main_call(basis.T, momentum, gradient)
    new_weight, new_momentum, new_basis_t = out_call(ortho, right, sums, momentum, gradient, weight)
    return new_weight, new_momentum, new_basis_t.T


def solution(mesh):
    return jax.shard_map(
        local,
        mesh=mesh,
        in_specs=(P("row", "col"), P("row", "col"), P("row", "col"), P("col", "row")),
        out_specs=(P("row", "col"), P("row", "col"), P("col", "row")),
        check_vma=False,
    )
```

```python
import math

import jax
import jax.numpy as jnp
from jax import lax
from jax.experimental import pallas as pl
from jax.experimental.pallas import tpu as pltpu
from jax.sharding import PartitionSpec as P

D = 8192
FF = 28672
RANK = 512
ROWS = 16
COLS = 32
TILES = 5
LIMIT = 53 * 2**20
F32 = jnp.float32
BF16 = jnp.bfloat16
MESH = pl.DeviceIdType.MESH
VMEM = pl.BlockSpec(memory_space=pltpu.VMEM)
ANY = pl.BlockSpec(memory_space=pl.ANY)
DMA = pltpu.SemaphoreType.DMA
NN = (((1,), (0,)), ((), ()))
NT = (((1,), (1,)), ((), ()))
TN = (((0,), (0,)), ((), ()))


def remote(src, dst, send, recv, **where):
    return pltpu.make_async_remote_copy(
        src_ref=src, dst_ref=dst, send_sem=send, recv_sem=recv, device_id=where, device_id_type=MESH)


def wait_bytes(ref, sem):
    pltpu.make_async_copy(ref, ref, sem).wait()


def ring(a):
    return lax.rem(a + 2 * ROWS, ROWS)


def greet(r, c):
    barrier = pltpu.get_barrier_semaphore()
    for k in (1, 2, ROWS - 1, ROWS - 2):
        pl.semaphore_signal(barrier, inc=1, device_id={"row": ring(r + k)}, device_id_type=MESH)

    def one(k, carry):
        pl.semaphore_signal(barrier, inc=1, device_id={"col": lax.rem(c + k, COLS)}, device_id_type=MESH)
        return carry

    lax.fori_loop(1, COLS, one, 0)
    return barrier, 4 + COLS - 1


def col_send(c, src_of, dst, send, recv):
    def one(k, carry):
        d = lax.rem(c + k, COLS)
        remote(src_of(d), dst, send, recv, col=d).start()
        return carry

    lax.fori_loop(1, COLS, one, 0)


class Gather:
    def __init__(self, r, buf, send, recv):
        self.r, self.buf, self.send, self.recv = r, buf, send, recv

    def message(self, way, d, h):
        sign = 1 if way == 0 else -1
        step = jnp.minimum(d, 2)
        block = self.buf.at[ring(self.r - sign * (d - step)), pl.ds(16 * h, 16), :]
        return remote(block, block, self.send.at[way, d, h], self.recv.at[way, d, h], row=ring(self.r + sign * step))

    def start(self):
        for d in (1, 2):
            for h in range(2):
                for way in range(2):
                    self.message(way, d, h).start()

    def forward(self, d):
        for h in range(2):
            for way in range(2):
                self.message(way, d, h).wait_recv()

                @pl.when(d + 2 <= 8 - way)
                def _():
                    self.message(way, d + 2, h).start()

    def end(self, d):
        for h in range(2):
            self.message(0, d, h).wait_recv()

            @pl.when(d <= 7)
            def _():
                self.message(1, d, h).wait_recv()

    def drain(self):
        def one(d, carry):
            for h in range(2):
                self.message(0, d, h).wait_send()

                @pl.when(d <= 7)
                def _():
                    self.message(1, d, h).wait_send()

            return carry

        lax.fori_loop(1, 9, one, 0)


class Reduce:
    def __init__(self, r, part, slots, first, send, recv):
        self.r, self.part, self.slots, self.first, self.send, self.recv = r, part, slots, first, send, recv
        self.size = RANK // ROWS

    def own(self, block, h):
        return self.part[pl.ds(pl.multiple_of(block * self.size + 16 * h, 16), 16), :]

    def message(self, way, d, h, src=None):
        sign = 1 if way == 0 else -1
        slot = self.slots.at[way, d, pl.ds(16 * h, 16), :]
        return remote(
            slot if src is None else src, slot, self.send.at[way, d, h], self.recv.at[way, d, h],
            row=ring(self.r + sign * jnp.minimum(d, 2)))

    def start(self):
        for i in range(2):
            for h in range(2):
                for way in range(2):
                    d = 8 - way - i
                    here = self.first.at[way, i, pl.ds(16 * h, 16), :]
                    here[...] = self.own(ring(self.r + (d if way == 0 else -d)), h).astype(BF16)
                    self.message(way, d, h, here).start()

    def forward(self, k):
        for h in range(2):
            for way in range(2):
                def go():
                    d = 6 - way - k
                    got = self.slots.at[way, d + 2, pl.ds(16 * h, 16), :]
                    self.message(way, d + 2, h).wait_recv()
                    term = self.own(ring(self.r + (d if way == 0 else -d)), h)
                    got[...] = (got[...].astype(F32) + term).astype(BF16)
                    self.message(way, d, h, got).start()

                if way == 0:
                    go()
                else:
                    pl.when(k < 5)(go)

    def end(self, h):
        total = self.own(self.r, h)
        for way in range(2):
            for d in (2, 1):
                self.message(way, d, h).wait_recv()
                total = total + self.slots[way, d, pl.ds(16 * h, 16), :].astype(F32)
        return total

    def drain(self):
        def one(d, carry):
            for h in range(2):
                self.message(0, d, h).wait_send()

                @pl.when(d <= 7)
                def _():
                    self.message(1, d, h).wait_send()

            return carry

        lax.fori_loop(1, 9, one, 0)


def split(x):
    high = x.astype(BF16)
    return high, (x - high.astype(F32)).astype(BF16)


def parts(x):
    high = x.astype(BF16)
    rest = x - high.astype(F32)
    mid = rest.astype(BF16)
    low = (rest - mid.astype(F32)).astype(BF16)
    return (high, high, mid, high, low, mid), (high, mid, high, low, high, mid)


def dot_exact(a, b):
    return lax.dot_general(
        jnp.concatenate(parts(a)[0], axis=0), jnp.concatenate(parts(b)[1], axis=0), TN, preferred_element_type=F32)


def factor_block(w, spare):
    sub = lax.broadcasted_iota(jnp.int32, (8, 256), 0)
    near = 3

    def twice(x):
        return jnp.concatenate([x, x], axis=1)

    def column(x, k):
        return jnp.broadcast_to(x[:, k:k + 1], (8, 128))

    for p in range(16):
        panel = w[p]
        rows = [jnp.broadcast_to(w[p, k:k + 1, :], (8, 256)) for k in range(8)]
        s, u, root = {}, {}, {}
        for j in range(8):
            spare[p % 2, j] = column(panel, 8 * p + j)
            for i in range(j + 1):
                s[i, j] = jnp.broadcast_to(spare[p % 2, j, i:i + 1, :], (8, 128))
        for j in range(8):
            root[j] = lax.rsqrt(s[j, j])
            for i in range(j + 1, 8):
                u[j, i] = s[j, i] * root[j]
            for i in range(j + 1, 8):
                for l in range(i, 8):
                    s[i, l] = s[i, l] - u[j, i] * u[j, l]
        for j in range(8):
            rows[j] = rows[j] * twice(root[j])
            for i in range(j + 1, 8):
                rows[i] = rows[i] - twice(u[j, i]) * rows[j]
        for g in range(p + 1, min(16, p + 1 + near)):
            rest = w[g]
            x = [column(rest, 8 * p + k) for k in range(8)]
            for k in range(8):
                x[k] = x[k] * root[k]
                for l in range(k + 1, 8):
                    x[l] = x[l] - x[k] * u[k, l]
            taken = twice(x[0]) * rows[0]
            for k in range(1, 8):
                taken = taken + twice(x[k]) * rows[k]
            w[g] = rest - taken
        done = rows[7]
        for k in range(7):
            done = jnp.where(sub == k, rows[k], done)
        w[p] = done
        far = p + 1 + near
        if far < 16:
            taken = dot_exact(done[:, :128], done)
            w[far:] = w[far:] - taken.reshape(16, 8, 256)[far:]


def factor_rows(work, block, spare, b):
    rows = pl.ds(pl.multiple_of(128 * b, 128), 128)
    live = pl.ds(pl.multiple_of(128 * (b + 1), 128), 512)
    block[:, :, :128] = work[rows, rows].reshape(16, 8, 128)
    block[:, :, 128:] = unit(128).reshape(16, 8, 128)
    factor_block(block, spare)
    inverse = block[:, :, 128:].reshape(128, 128)
    panel = lax.dot_general(
        jnp.concatenate(parts(inverse)[0], axis=1), jnp.concatenate(parts(work[rows, live])[1], axis=0), NN,
        preferred_element_type=F32)
    work[rows, live] = panel

    @pl.when(b < 3)
    def _():
        below = pl.ds(pl.multiple_of(128 * (b + 1), 128), 384)
        work[below, live] = work[below, live] - dot_exact(panel[:, :384], panel)


def unit(rows):
    return jnp.where(
        lax.broadcasted_iota(jnp.int32, (rows, rows), 0) == lax.broadcasted_iota(jnp.int32, (rows, rows), 1), 1.0, 0.0)


def main_kernel(
    basis_in, momentum, gradient, weight, ortho_out, basis_out, momentum_out, weight_out,
    basis_all, loaded, buffer, partial, arrived, lefts, left, order, cross_part, slots, first, cross_all,
    gram_part, gram_send, gram_recv, gram_tiles, gram_all, work, block, spare, sums,
    load_sems, basis_send, basis_recv, red_send, red_recv, cross_send, cross_recv, left_sems, sems,
):
    r, c = lax.axis_index("row"), lax.axis_index("col")
    core = lax.rem(c, 2)
    barrier, count = greet(r, c)
    loads = [
        pltpu.make_async_copy(basis_in, basis_all.at[r], load_sems.at[0]),
        pltpu.make_async_copy(momentum, loaded.at[0], load_sems.at[1]),
        pltpu.make_async_copy(gradient, loaded.at[1], load_sems.at[2]),
    ]
    for load in loads:
        load.start()
    keep = pltpu.make_async_copy(weight, weight_out, load_sems.at[3])
    keep.start()
    work[...] = jnp.zeros((896, 1024), F32)
    for b in range(4):
        work[128 * b:128 * b + 128, 512 + 128 * b:512 + 128 * b + 128] = unit(128)
    place = lax.broadcasted_iota(jnp.int32, (512, 512), 0)
    turn = (place >> 5) & 3
    far = 2 * (place >> 7) + 1 + (turn >> 1)
    source = jnp.where(place >= 480, r, jnp.where((turn & 1) == 0, r - far, r + far)) & (ROWS - 1)
    natural = source * 32 + (place & 31)
    order[...] = jnp.where(natural == lax.broadcasted_iota(jnp.int32, (512, 512), 1), 1.0, 0.0).astype(BF16)
    for load in loads:
        load.wait()
    buffer[...] = (loaded[0].astype(F32) + loaded[1].astype(F32)).astype(BF16)
    pl.semaphore_wait(barrier, count)

    gather = Gather(r, basis_all, basis_send, basis_recv)
    gather.start()

    def send_partial(w):
        if w < 3:
            for d in (2 * w + 1, 2 * w + 2):
                gather.forward(d)
            ids = [r - (2 * w + 1), r + (2 * w + 1), r - (2 * w + 2), r + (2 * w + 2)]
        else:
            gather.end(7)
            gather.end(8)
            ids = [r - 7, r + 7, r - 8, r]
        columns = jnp.concatenate([basis_all[ring(i)] for i in ids], axis=0)
        partial[w] = lax.dot_general(buffer[...], columns, NT, preferred_element_type=F32).astype(BF16)

        def rows_of(d):
            return partial.at[w, pl.ds(pl.multiple_of(d * 16, 16), 16), :]

        col_send(c, rows_of, arrived.at[w, c], left_sems.at[0, w], left_sems.at[1, w])
        arrived[w, c] = rows_of(c)[...]

    def send_left(w):
        wait_bytes(arrived.at[w, pl.ds(0, COLS - 1)], left_sems.at[1, w])
        total = arrived[w, 0].astype(F32)
        for k in range(1, COLS):
            total = total + arrived[w, k].astype(F32)
        lefts[w, c] = total.astype(BF16)
        col_send(c, lambda d: lefts.at[w, c], lefts.at[w, c], left_sems.at[2, w], left_sems.at[3, w])

    for w in range(4):
        send_partial(w)
        if w > 0:
            send_left(w - 1)
    send_left(3)
    for w in range(4):
        wait_bytes(arrived.at[w, pl.ds(0, COLS - 1)], left_sems.at[3, w])
    mixed = jnp.concatenate([lefts[w].reshape(512, 128) for w in range(4)], axis=1)
    left[...] = jnp.dot(mixed, order[...], preferred_element_type=F32).astype(BF16)

    quarter = c // 16
    for i in range(2):
        start = quarter if i == 0 else 3 - quarter
        lanes = left[:, pl.ds(pl.multiple_of(start * 128, 128), 128)]
        gram_part[i] = lax.dot_general(lanes, left[...], TN, preferred_element_type=F32)
    low = lax.rem(c, 16)
    for t in range(TILES):
        upper = t < 4 - quarter
        part = jnp.where(upper, 0, 1)
        row = jnp.where(upper, low, 15 - low)
        lane = jnp.where(upper, t + quarter, t - 1)
        gram_send[t] = gram_part[part, pl.ds(pl.multiple_of(row * 8, 8), 8), pl.ds(pl.multiple_of(lane * 128, 128), 128)]

    mine = lax.rem(r, 8)
    reducer = mine < TILES

    def send_tile(k, carry):
        d = ring(r + k)
        t = lax.rem(d, 8)

        @pl.when(t < TILES)
        def _():
            remote(gram_send.at[t], gram_recv.at[r], sems.at[0], sems.at[1], row=d).start()

        return carry

    lax.fori_loop(1, ROWS, send_tile, 0)

    for n in range(2):
        cross_part[256 * n:256 * n + 256, :] = lax.dot_general(
            left[:, 256 * n:256 * n + 256], buffer[...], TN, preferred_element_type=F32)
    reduce = Reduce(r, cross_part, slots, first, red_send, red_recv)
    reduce.start()

    @pl.when(reducer)
    def _():
        wait_bytes(gram_recv.at[pl.ds(0, ROWS - 1)], sems.at[1])
        gram_recv[r] = gram_send[mine]
        tile = gram_recv[0]
        for k in range(1, ROWS):
            tile = tile + gram_recv[k]
        gram_tiles[mine] = tile
        for k in (-3, -2, -1, 1, 2, 3, 4):
            remote(gram_tiles.at[mine], gram_tiles.at[mine], sems.at[2], sems.at[3], row=ring(r + k)).start()

    for k in range(2):
        reduce.forward(k)

    @pl.when(reducer)
    def _():
        wait_bytes(gram_recv.at[pl.ds(0, TILES - 1)], sems.at[3])

    @pl.when(jnp.logical_not(reducer))
    def _():
        wait_bytes(gram_recv.at[pl.ds(0, TILES)], sems.at[3])

    chip = c // 2
    gram_all[core, chip] = gram_tiles[...]

    def send_gram(k, carry):
        remote(gram_all.at[core, chip], gram_all.at[core, chip], sems.at[4], sems.at[5],
               col=lax.rem(c + 2 * k, COLS)).start()
        return carry

    lax.fori_loop(1, COLS // 2, send_gram, 0)
    for k in range(2, 4):
        reduce.forward(k)
    wait_bytes(gram_all.at[0, pl.ds(0, 15)], sems.at[5])
    sibling = remote(gram_all.at[core], gram_all.at[core], sems.at[6], sems.at[7], col=c + 1 - 2 * core)
    sibling.start()
    for k in range(4, 6):
        reduce.forward(k)
    sibling.wait_recv()

    def place_tiles(k, carry):
        kc = 2 * (k // 2) + lax.rem(k, 2)
        kq = kc // 16
        for t in range(TILES):
            upper = t < 4 - kq
            row = jnp.where(upper, kc, 63 - kc)
            lane = jnp.where(upper, t + kq, t - 1)
            work[pl.ds(pl.multiple_of(row * 8, 8), 8), pl.ds(pl.multiple_of(lane * 128, 128), 128)] = (
                gram_all[lax.rem(k, 2), k // 2, t])
        return carry

    lax.fori_loop(0, COLS, place_tiles, 0)
    for h in range(2):
        cross_all[r, pl.ds(16 * h, 16), :] = reduce.end(h).astype(BF16)
    spread = Gather(r, cross_all, cross_send, cross_recv)
    spread.start()

    def factor_step(b, carry):
        factor_rows(work, block, spare, b)

        @pl.when(b < 3)
        def _():
            spread.forward(2 * b + 1)
            spread.forward(2 * b + 2)

        return carry

    lax.fori_loop(0, 4, factor_step, 0)
    spread.end(7)
    spread.end(8)

    high, low_part = split(work[:512, 512:])
    cross = cross_all[...].reshape(512, 896)
    right = jnp.dot(high, cross, preferred_element_type=F32) + jnp.dot(low_part, cross, preferred_element_type=F32)
    square_high, square_low = split(right * right)
    ones = jnp.ones((8, 896), BF16)
    total = (
        lax.dot_general(ones, square_high, NT, preferred_element_type=F32)
        + lax.dot_general(ones, square_low, NT, preferred_element_type=F32))
    sub = lax.broadcasted_iota(jnp.int32, (8, 128), 0)
    tile = total[:, :128]
    for q in range(1, 4):
        tile = jnp.where(sub == q, total[:, 128 * q:128 * q + 128], tile)
    sums[c] = tile
    col_send(c, lambda d: sums.at[c], sums.at[c], sems.at[8], sems.at[9])
    ortho = (
        lax.dot_general(left[...], high, NT, preferred_element_type=F32)
        + lax.dot_general(left[...], low_part, NT, preferred_element_type=F32)).astype(BF16)
    ortho_out[...] = ortho
    correction = jnp.dot(ortho, right.astype(BF16), preferred_element_type=F32)
    momentum_out[...] = (buffer[...].astype(F32) - 0.2 * correction).astype(BF16)
    keep.wait()

    gather.drain()
    reduce.drain()
    spread.drain()
    for w in range(4):
        wait_bytes(arrived.at[w, pl.ds(0, COLS - 1)], left_sems.at[0, w])
        wait_bytes(arrived.at[w, pl.ds(0, COLS - 1)], left_sems.at[2, w])

    @pl.when(reducer)
    def _():
        wait_bytes(gram_recv.at[pl.ds(0, 2 * TILES - 1)], sems.at[0])
        wait_bytes(gram_recv.at[pl.ds(0, 7)], sems.at[2])

    @pl.when(jnp.logical_not(reducer))
    def _():
        wait_bytes(gram_recv.at[pl.ds(0, 2 * TILES)], sems.at[0])

    wait_bytes(gram_all.at[0, pl.ds(0, 15)], sems.at[4])
    sibling.wait_send()
    wait_bytes(sums.at[pl.ds(0, COLS - 1)], sems.at[8])
    wait_bytes(sums.at[pl.ds(0, COLS - 1)], sems.at[9])
    total = sums[0]
    for k in range(1, COLS):
        total = total + sums[k]
    scale = lax.rsqrt(total / FF + 1e-06).T
    for q in range(4):
        basis_out[128 * q:128 * q + 128, :] = (right[128 * q:128 * q + 128, :] * scale[:, q:q + 1]).astype(BF16)


def main_call(basis_t, momentum, gradient, weight):
    return pl.pallas_call(
        main_kernel,
        out_shape=[
            jax.ShapeDtypeStruct((512, 512), BF16),
            jax.ShapeDtypeStruct((512, 896), BF16),
            jax.ShapeDtypeStruct((512, 896), BF16),
            jax.ShapeDtypeStruct((512, 896), BF16),
        ],
        in_specs=[ANY] * 4,
        out_specs=[VMEM] * 4,
        scratch_shapes=[
            pltpu.VMEM((ROWS, 32, 896), BF16),
            pltpu.VMEM((2, 512, 896), BF16),
            pltpu.VMEM((512, 896), BF16),
            pltpu.VMEM((4, 512, 128), BF16),
            pltpu.VMEM((4, COLS, 16, 128), BF16),
            pltpu.VMEM((4, COLS, 16, 128), BF16),
            pltpu.VMEM((512, 512), BF16),
            pltpu.VMEM((512, 512), BF16),
            pltpu.VMEM((512, 896), F32),
            pltpu.VMEM((2, 9, 32, 896), BF16),
            pltpu.VMEM((2, 2, 32, 896), BF16),
            pltpu.VMEM((ROWS, 32, 896), BF16),
            pltpu.VMEM((2, 128, 512), F32),
            pltpu.VMEM((TILES, 8, 128), F32),
            pltpu.VMEM((ROWS, 8, 128), F32),
            pltpu.VMEM((TILES, 8, 128), F32),
            pltpu.VMEM((2, COLS // 2, TILES, 8, 128), F32),
            pltpu.VMEM((896, 1024), F32),
            pltpu.VMEM((16, 8, 256), F32),
            pltpu.VMEM((2, 8, 8, 128), F32),
            pltpu.VMEM((COLS, 8, 128), F32),
            DMA((4,)),
            DMA((2, 9, 2)), DMA((2, 9, 2)),
            DMA((2, 9, 2)), DMA((2, 9, 2)),
            DMA((2, 9, 2)), DMA((2, 9, 2)),
            DMA((4, 4)),
            DMA((10,)),
        ],
        compiler_params=pltpu.CompilerParams(
            collective_id=0, has_side_effects=True, vmem_limit_bytes=LIMIT),
    )(basis_t, momentum, gradient, weight)


def out_kernel(ortho, basis, momentum, weight, new_weight, new_momentum, new_basis_t, done, sems):
    r = lax.axis_index("row")
    copies = [
        pltpu.make_async_copy(momentum, new_momentum, sems.at[0]),
        pltpu.make_async_copy(basis.at[pl.ds(pl.multiple_of(r * 32, 32), 32), :], new_basis_t, sems.at[1]),
    ]
    for copy in copies:
        copy.start()
    for q in range(4):
        rows = pl.ds(128 * q, 128)
        update = jnp.dot(ortho[rows, :], basis[...], preferred_element_type=F32)
        done[rows, :] = (weight[rows, :].astype(F32) - 0.5 * math.sqrt(D / RANK) * update).astype(BF16)
        copies.append(pltpu.make_async_copy(done.at[rows, :], new_weight.at[rows, :], sems.at[2 + q]))
        copies[2 + q].start()
    for copy in copies:
        copy.wait()


def out_call(ortho, basis, momentum, weight):
    return pl.pallas_call(
        out_kernel,
        out_shape=[
            jax.ShapeDtypeStruct((512, 896), BF16),
            jax.ShapeDtypeStruct((512, 896), BF16),
            jax.ShapeDtypeStruct((32, 896), BF16),
        ],
        in_specs=[VMEM] * 4,
        out_specs=[ANY] * 3,
        scratch_shapes=[pltpu.VMEM((512, 896), BF16), DMA((6,))],
        compiler_params=pltpu.CompilerParams(vmem_limit_bytes=LIMIT),
    )(ortho, basis, momentum, weight)


def local(weight, gradient, momentum, basis):
    outputs = out_call(*main_call(basis.T, momentum, gradient, weight))
    return outputs[0], outputs[1], outputs[2].T


def solution(mesh):
    return jax.shard_map(
        local,
        mesh=mesh,
        in_specs=(P("row", "col"), P("row", "col"), P("row", "col"), P("col", "row")),
        out_specs=(P("row", "col"), P("row", "col"), P("col", "row")),
        check_vma=False,
    )
```

```python
import math

import jax
import jax.numpy as jnp
from jax import lax
from jax.experimental import pallas as pl
from jax.experimental.pallas import tpu as pltpu
from jax.sharding import PartitionSpec as P

D = 8192
FF = 28672
RANK = 512
ROWS = 16
COLS = 32
TILES = 5
LIMIT = 53 * 2**20
F32 = jnp.float32
BF16 = jnp.bfloat16
MESH = pl.DeviceIdType.MESH
VMEM = pl.BlockSpec(memory_space=pltpu.VMEM)
ANY = pl.BlockSpec(memory_space=pl.ANY)
DMA = pltpu.SemaphoreType.DMA
NN = (((1,), (0,)), ((), ()))
NT = (((1,), (1,)), ((), ()))
TN = (((0,), (0,)), ((), ()))


def remote(src, dst, send, recv, **where):
    return pltpu.make_async_remote_copy(
        src_ref=src, dst_ref=dst, send_sem=send, recv_sem=recv, device_id=where, device_id_type=MESH)


def wait_bytes(ref, sem):
    pltpu.make_async_copy(ref, ref, sem).wait()


def ring(a):
    return lax.rem(a + 2 * ROWS, ROWS)


def greet(r, c):
    barrier = pltpu.get_barrier_semaphore()
    for k in (1, 2, ROWS - 1, ROWS - 2):
        pl.semaphore_signal(barrier, inc=1, device_id={"row": ring(r + k)}, device_id_type=MESH)

    def one(k, carry):
        pl.semaphore_signal(barrier, inc=1, device_id={"col": lax.rem(c + k, COLS)}, device_id_type=MESH)
        return carry

    lax.fori_loop(1, COLS, one, 0)
    return barrier, 4 + COLS - 1


def col_send(c, src_of, dst, send, recv):
    def one(k, carry):
        d = lax.rem(c + 1 + lax.rem(k + COLS // 2 - 1, COLS - 1), COLS)
        remote(src_of(d), dst, send, recv, col=d).start()
        return carry

    lax.fori_loop(0, COLS - 1, one, 0)


class Gather:
    def __init__(self, r, buf, send, recv):
        self.r, self.buf, self.send, self.recv = r, buf, send, recv

    def message(self, way, d, h):
        sign = 1 if way == 0 else -1
        step = 2 - d % 2
        block = self.buf.at[ring(self.r - sign * (d - step)), pl.ds(16 * h, 16), :]
        return remote(block, block, self.send.at[way, d, h], self.recv.at[way, d, h], row=ring(self.r + sign * step))

    def start(self):
        for d in (2, 1):
            for h in range(2):
                for way in range(2):
                    self.message(way, d, h).start()

    def forward(self, d):
        for h in range(2):
            for way in range(2):
                self.message(way, d, h).wait_recv()
                if d + 2 <= 8 - way:
                    self.message(way, d + 2, h).start()
                self.message(way, d + 1, h).start()

    def end(self, d):
        for h in range(2):
            for way in range(2):
                if d <= 8 - way:
                    self.message(way, d, h).wait_recv()

    def drain(self):
        for d in range(1, 9):
            for h in range(2):
                for way in range(2):
                    if d <= 8 - way:
                        self.message(way, d, h).wait_send()


class Reduce:
    def __init__(self, r, part, slots, first, send, recv):
        self.r, self.part, self.slots, self.first, self.send, self.recv = r, part, slots, first, send, recv
        self.size = RANK // ROWS

    def own(self, way, d, h):
        block = ring(self.r + (d if way == 0 else -d))
        return self.part[pl.ds(pl.multiple_of(block * self.size + 16 * h, 16), 16), :]

    def slot(self, way, d, h):
        return self.slots.at[way, d, pl.ds(16 * h, 16), :]

    def message(self, way, d, h, src=None):
        sign = 1 if way == 0 else -1
        slot = self.slot(way, d, h)
        return remote(
            slot if src is None else src, slot, self.send.at[way, d, h], self.recv.at[way, d, h],
            row=ring(self.r + sign * (2 - d % 2)))

    def give(self, way, d, h):
        here = self.first.at[way, d // 2, pl.ds(16 * h, 16), :]
        here[...] = self.own(way, d, h).astype(BF16)
        self.message(way, d, h, here).start()

    def start(self):
        for h in range(2):
            self.give(0, 8, h)
            self.give(1, 7, h)
            self.give(0, 7, h)

    def forward(self, d):
        for h in range(2):
            for way in range(2):
                total = self.own(way, d, h)
                for far in (d + 1, d + 2):
                    if far <= 8 - way:
                        self.message(way, far, h).wait_recv()
                        total = total + self.slot(way, far, h)[...].astype(F32)
                here = self.slot(way, d + 1, h)
                here[...] = total.astype(BF16)
                self.message(way, d, h, here).start()
                self.give(way, d - 1, h)

    def end(self, h):
        total = self.own(0, 0, h)
        for way in range(2):
            for d in (1, 2):
                self.message(way, d, h).wait_recv()
                total = total + self.slot(way, d, h)[...].astype(F32)
        return total

    def drain(self):
        for d in range(1, 9):
            for h in range(2):
                for way in range(2):
                    if d <= 8 - way:
                        self.message(way, d, h).wait_send()


def split(x):
    high = x.astype(BF16)
    return high, (x - high.astype(F32)).astype(BF16)


def parts(x):
    high = x.astype(BF16)
    rest = x - high.astype(F32)
    mid = rest.astype(BF16)
    low = (rest - mid.astype(F32)).astype(BF16)
    return (high, high, mid, high, low, mid), (high, mid, high, low, high, mid)


def dot_exact(a, b):
    return lax.dot_general(
        jnp.concatenate(parts(a)[0], axis=0), jnp.concatenate(parts(b)[1], axis=0), TN, preferred_element_type=F32)


def factor_block(w, spare, midway):
    sub = lax.broadcasted_iota(jnp.int32, (8, 256), 0)
    near = 3

    def twice(x):
        return jnp.concatenate([x, x], axis=1)

    def column(x, k):
        return jnp.broadcast_to(x[:, k:k + 1], (8, 128))

    for p in range(16):
        if p == 8:
            midway()
        panel = w[p]
        rows = [jnp.broadcast_to(w[p, k:k + 1, :], (8, 256)) for k in range(8)]
        s, u, root = {}, {}, {}
        for j in range(8):
            spare[p % 2, j] = column(panel, 8 * p + j)
            for i in range(j + 1):
                s[i, j] = jnp.broadcast_to(spare[p % 2, j, i:i + 1, :], (8, 128))
        for j in range(8):
            root[j] = lax.rsqrt(s[j, j])
            for i in range(j + 1, 8):
                u[j, i] = s[j, i] * root[j]
            for i in range(j + 1, 8):
                for l in range(i, 8):
                    s[i, l] = s[i, l] - u[j, i] * u[j, l]
        for j in range(8):
            rows[j] = rows[j] * twice(root[j])
            for i in range(j + 1, 8):
                rows[i] = rows[i] - twice(u[j, i]) * rows[j]
        for g in range(p + 1, min(16, p + 1 + near)):
            rest = w[g]
            x = [column(rest, 8 * p + k) for k in range(8)]
            for k in range(8):
                x[k] = x[k] * root[k]
                for l in range(k + 1, 8):
                    x[l] = x[l] - x[k] * u[k, l]
            taken = twice(x[0]) * rows[0]
            for k in range(1, 8):
                taken = taken + twice(x[k]) * rows[k]
            w[g] = rest - taken
        done = rows[7]
        for k in range(7):
            done = jnp.where(sub == k, rows[k], done)
        w[p] = done
        far = p + 1 + near
        if far < 16:
            taken = dot_exact(done[:, :128], done)
            w[far:] = w[far:] - taken.reshape(16, 8, 256)[far:]


def factor_rows(work, block, spare, b, midway):
    rows = pl.ds(pl.multiple_of(128 * b, 128), 128)
    live = pl.ds(pl.multiple_of(128 * (b + 1), 128), 512)
    block[:, :, :128] = work[rows, rows].reshape(16, 8, 128)
    block[:, :, 128:] = unit(128).reshape(16, 8, 128)
    factor_block(block, spare, midway)
    inverse = block[:, :, 128:].reshape(128, 128)
    panel = lax.dot_general(
        jnp.concatenate(parts(inverse)[0], axis=1), jnp.concatenate(parts(work[rows, live])[1], axis=0), NN,
        preferred_element_type=F32)
    work[rows, live] = panel

    @pl.when(b < 3)
    def _():
        below = pl.ds(pl.multiple_of(128 * (b + 1), 128), 384)
        work[below, live] = work[below, live] - dot_exact(panel[:, :384], panel)


def unit(rows):
    return jnp.where(
        lax.broadcasted_iota(jnp.int32, (rows, rows), 0) == lax.broadcasted_iota(jnp.int32, (rows, rows), 1), 1.0, 0.0)


def main_kernel(
    basis_in, momentum, gradient, weight, ortho_out, basis_out, momentum_out, weight_out,
    basis_all, loaded, buffer, partial, arrived, lefts, left, order, cross_part, slots, first, cross_all,
    gram_part, gram_send, gram_recv, gram_tiles, gram_all, work, block, spare, sums,
    load_sems, basis_send, basis_recv, red_send, red_recv, cross_send, cross_recv, left_sems, sems,
):
    r, c = lax.axis_index("row"), lax.axis_index("col")
    core = lax.rem(c, 2)
    barrier, count = greet(r, c)
    loads = [
        pltpu.make_async_copy(basis_in, basis_all.at[r], load_sems.at[0]),
        pltpu.make_async_copy(momentum, loaded.at[0], load_sems.at[1]),
        pltpu.make_async_copy(gradient, loaded.at[1], load_sems.at[2]),
    ]
    for load in loads:
        load.start()
    keep = pltpu.make_async_copy(weight, weight_out, load_sems.at[3])
    keep.start()
    work[...] = jnp.zeros((896, 1024), F32)
    for b in range(4):
        work[128 * b:128 * b + 128, 512 + 128 * b:512 + 128 * b + 128] = unit(128)
    place = lax.broadcasted_iota(jnp.int32, (512, 512), 0)
    turn = (place >> 5) & 3
    far = 2 * (place >> 7) + 1 + (turn >> 1)
    source = jnp.where(place >= 480, r, jnp.where((turn & 1) == 0, r - far, r + far)) & (ROWS - 1)
    natural = source * 32 + (place & 31)
    order[...] = jnp.where(natural == lax.broadcasted_iota(jnp.int32, (512, 512), 1), 1.0, 0.0).astype(BF16)
    for load in loads:
        load.wait()
    buffer[...] = (loaded[0].astype(F32) + loaded[1].astype(F32)).astype(BF16)
    pl.semaphore_wait(barrier, count)

    gather = Gather(r, basis_all, basis_send, basis_recv)
    gather.start()

    def send_partial(w):
        if w < 3:
            gather.forward(2 * w + 2)
            gather.end(2 * w + 1)
            ids = [r - (2 * w + 1), r + (2 * w + 1), r - (2 * w + 2), r + (2 * w + 2)]
        else:
            gather.end(7)
            gather.end(8)
            ids = [r - 7, r + 7, r - 8, r]
        columns = jnp.concatenate([basis_all[ring(i)] for i in ids], axis=0)
        partial[w] = lax.dot_general(buffer[...], columns, NT, preferred_element_type=F32).astype(BF16)

        def rows_of(d):
            return partial.at[w, pl.ds(pl.multiple_of(d * 16, 16), 16), :]

        col_send(c, rows_of, arrived.at[w, c], left_sems.at[0, w], left_sems.at[1, w])
        arrived[w, c] = rows_of(c)[...]

    def send_left(w):
        wait_bytes(arrived.at[w, pl.ds(0, COLS - 1)], left_sems.at[1, w])
        total = arrived[w, 0].astype(F32)
        for k in range(1, COLS):
            total = total + arrived[w, k].astype(F32)
        lefts[w, c] = total.astype(BF16)
        col_send(c, lambda d: lefts.at[w, c], lefts.at[w, c], left_sems.at[2, w], left_sems.at[3, w])

    for w in range(4):
        send_partial(w)
        if w > 0:
            send_left(w - 1)
    send_left(3)
    for w in range(4):
        wait_bytes(arrived.at[w, pl.ds(0, COLS - 1)], left_sems.at[3, w])
    mixed = jnp.concatenate([lefts[w].reshape(512, 128) for w in range(4)], axis=1)
    left[...] = jnp.dot(mixed, order[...], preferred_element_type=F32).astype(BF16)

    quarter = c // 16
    for i in range(2):
        start = quarter if i == 0 else 3 - quarter
        lanes = left[:, pl.ds(pl.multiple_of(start * 128, 128), 128)]
        gram_part[i] = lax.dot_general(lanes, left[...], TN, preferred_element_type=F32)
    low = lax.rem(c, 16)
    for t in range(TILES):
        upper = t < 4 - quarter
        part = jnp.where(upper, 0, 1)
        row = jnp.where(upper, low, 15 - low)
        lane = jnp.where(upper, t + quarter, t - 1)
        gram_send[t] = gram_part[part, pl.ds(pl.multiple_of(row * 8, 8), 8), pl.ds(pl.multiple_of(lane * 128, 128), 128)]

    mine = lax.rem(r, 8)
    reducer = mine < TILES

    def send_tile(k, carry):
        d = ring(r + k)
        t = lax.rem(d, 8)

        @pl.when(t < TILES)
        def _():
            remote(gram_send.at[t], gram_recv.at[r], sems.at[0], sems.at[1], row=d).start()

        return carry

    lax.fori_loop(1, ROWS, send_tile, 0)

    for n in range(2):
        cross_part[256 * n:256 * n + 256, :] = lax.dot_general(
            left[:, 256 * n:256 * n + 256], buffer[...], TN, preferred_element_type=F32)
    reduce = Reduce(r, cross_part, slots, first, red_send, red_recv)
    reduce.start()
    reduce.forward(6)

    @pl.when(reducer)
    def _():
        wait_bytes(gram_recv.at[pl.ds(0, ROWS - 1)], sems.at[1])
        gram_recv[r] = gram_send[mine]
        tile = gram_recv[0]
        for k in range(1, ROWS):
            tile = tile + gram_recv[k]
        gram_tiles[mine] = tile
        for k in (-3, -2, -1, 1, 2, 3, 4):
            remote(gram_tiles.at[mine], gram_tiles.at[mine], sems.at[2], sems.at[3], row=ring(r + k)).start()

    reduce.forward(4)

    @pl.when(reducer)
    def _():
        wait_bytes(gram_recv.at[pl.ds(0, TILES - 1)], sems.at[3])

    @pl.when(jnp.logical_not(reducer))
    def _():
        wait_bytes(gram_recv.at[pl.ds(0, TILES)], sems.at[3])

    chip = c // 2
    gram_all[core, chip] = gram_tiles[...]

    def send_gram(k, carry):
        remote(gram_all.at[core, chip], gram_all.at[core, chip], sems.at[4], sems.at[5],
               col=lax.rem(c + 2 * k, COLS)).start()
        return carry

    lax.fori_loop(1, COLS // 2, send_gram, 0)
    reduce.forward(2)
    wait_bytes(gram_all.at[0, pl.ds(0, 15)], sems.at[5])
    sibling = remote(gram_all.at[core], gram_all.at[core], sems.at[6], sems.at[7], col=c + 1 - 2 * core)
    sibling.start()
    sibling.wait_recv()

    def place_tiles(k, carry):
        kc = 2 * (k // 2) + lax.rem(k, 2)
        kq = kc // 16
        for t in range(TILES):
            upper = t < 4 - kq
            row = jnp.where(upper, kc, 63 - kc)
            lane = jnp.where(upper, t + kq, t - 1)
            work[pl.ds(pl.multiple_of(row * 8, 8), 8), pl.ds(pl.multiple_of(lane * 128, 128), 128)] = (
                gram_all[lax.rem(k, 2), k // 2, t])
        return carry

    lax.fori_loop(0, COLS, place_tiles, 0)
    spread = Gather(r, cross_all, cross_send, cross_recv)

    def factor_step(b, carry):
        def midway():
            @pl.when(b == 0)
            def _():
                for h in range(2):
                    cross_all[r, pl.ds(16 * h, 16), :] = reduce.end(h).astype(BF16)
                spread.start()

            @pl.when(b == 1)
            def _():
                spread.forward(2)

        factor_rows(work, block, spare, b, midway)

        @pl.when(b == 2)
        def _():
            spread.forward(4)

        return carry

    lax.fori_loop(0, 4, factor_step, 0)
    spread.forward(6)
    for d in (1, 3, 5, 7, 8):
        spread.end(d)

    high, low_part = split(work[:512, 512:])
    cross = cross_all[...].reshape(512, 896)
    right = jnp.dot(high, cross, preferred_element_type=F32) + jnp.dot(low_part, cross, preferred_element_type=F32)
    square_high, square_low = split(right * right)
    ones = jnp.ones((8, 896), BF16)
    total = (
        lax.dot_general(ones, square_high, NT, preferred_element_type=F32)
        + lax.dot_general(ones, square_low, NT, preferred_element_type=F32))
    sub = lax.broadcasted_iota(jnp.int32, (8, 128), 0)
    tile = total[:, :128]
    for q in range(1, 4):
        tile = jnp.where(sub == q, total[:, 128 * q:128 * q + 128], tile)
    sums[c] = tile
    col_send(c, lambda d: sums.at[c], sums.at[c], sems.at[8], sems.at[9])
    ortho = (
        lax.dot_general(left[...], high, NT, preferred_element_type=F32)
        + lax.dot_general(left[...], low_part, NT, preferred_element_type=F32)).astype(BF16)
    ortho_out[...] = ortho
    correction = jnp.dot(ortho, right.astype(BF16), preferred_element_type=F32)
    momentum_out[...] = (buffer[...].astype(F32) - 0.2 * correction).astype(BF16)
    keep.wait()

    gather.drain()
    reduce.drain()
    spread.drain()
    for w in range(4):
        wait_bytes(arrived.at[w, pl.ds(0, COLS - 1)], left_sems.at[0, w])
        wait_bytes(arrived.at[w, pl.ds(0, COLS - 1)], left_sems.at[2, w])

    @pl.when(reducer)
    def _():
        wait_bytes(gram_recv.at[pl.ds(0, 2 * TILES - 1)], sems.at[0])
        wait_bytes(gram_recv.at[pl.ds(0, 7)], sems.at[2])

    @pl.when(jnp.logical_not(reducer))
    def _():
        wait_bytes(gram_recv.at[pl.ds(0, 2 * TILES)], sems.at[0])

    wait_bytes(gram_all.at[0, pl.ds(0, 15)], sems.at[4])
    sibling.wait_send()
    wait_bytes(sums.at[pl.ds(0, COLS - 1)], sems.at[8])
    wait_bytes(sums.at[pl.ds(0, COLS - 1)], sems.at[9])
    total = sums[0]
    for k in range(1, COLS):
        total = total + sums[k]
    scale = lax.rsqrt(total / FF + 1e-06).T
    for q in range(4):
        basis_out[128 * q:128 * q + 128, :] = (right[128 * q:128 * q + 128, :] * scale[:, q:q + 1]).astype(BF16)


def main_call(basis_t, momentum, gradient, weight):
    return pl.pallas_call(
        main_kernel,
        out_shape=[
            jax.ShapeDtypeStruct((512, 512), BF16),
            jax.ShapeDtypeStruct((512, 896), BF16),
            jax.ShapeDtypeStruct((512, 896), BF16),
            jax.ShapeDtypeStruct((512, 896), BF16),
        ],
        in_specs=[ANY] * 4,
        out_specs=[VMEM] * 4,
        scratch_shapes=[
            pltpu.VMEM((ROWS, 32, 896), BF16),
            pltpu.VMEM((2, 512, 896), BF16),
            pltpu.VMEM((512, 896), BF16),
            pltpu.VMEM((4, 512, 128), BF16),
            pltpu.VMEM((4, COLS, 16, 128), BF16),
            pltpu.VMEM((4, COLS, 16, 128), BF16),
            pltpu.VMEM((512, 512), BF16),
            pltpu.VMEM((512, 512), BF16),
            pltpu.VMEM((512, 896), F32),
            pltpu.VMEM((2, 9, 32, 896), BF16),
            pltpu.VMEM((2, 5, 32, 896), BF16),
            pltpu.VMEM((ROWS, 32, 896), BF16),
            pltpu.VMEM((2, 128, 512), F32),
            pltpu.VMEM((TILES, 8, 128), F32),
            pltpu.VMEM((ROWS, 8, 128), F32),
            pltpu.VMEM((TILES, 8, 128), F32),
            pltpu.VMEM((2, COLS // 2, TILES, 8, 128), F32),
            pltpu.VMEM((896, 1024), F32),
            pltpu.VMEM((16, 8, 256), F32),
            pltpu.VMEM((2, 8, 8, 128), F32),
            pltpu.VMEM((COLS, 8, 128), F32),
            DMA((4,)),
            DMA((2, 9, 2)), DMA((2, 9, 2)),
            DMA((2, 9, 2)), DMA((2, 9, 2)),
            DMA((2, 9, 2)), DMA((2, 9, 2)),
            DMA((4, 4)),
            DMA((10,)),
        ],
        compiler_params=pltpu.CompilerParams(
            collective_id=0, has_side_effects=True, vmem_limit_bytes=LIMIT),
    )(basis_t, momentum, gradient, weight)


def out_kernel(ortho, basis, momentum, weight, new_weight, new_momentum, new_basis_t, done, sems):
    r = lax.axis_index("row")
    copies = [
        pltpu.make_async_copy(momentum, new_momentum, sems.at[0]),
        pltpu.make_async_copy(basis.at[pl.ds(pl.multiple_of(r * 32, 32), 32), :], new_basis_t, sems.at[1]),
    ]
    for copy in copies:
        copy.start()
    for q in range(4):
        rows = pl.ds(128 * q, 128)
        update = jnp.dot(ortho[rows, :], basis[...], preferred_element_type=F32)
        done[rows, :] = (weight[rows, :].astype(F32) - 0.5 * math.sqrt(D / RANK) * update).astype(BF16)
        copies.append(pltpu.make_async_copy(done.at[rows, :], new_weight.at[rows, :], sems.at[2 + q]))
        copies[2 + q].start()
    for copy in copies:
        copy.wait()


def out_call(ortho, basis, momentum, weight):
    return pl.pallas_call(
        out_kernel,
        out_shape=[
            jax.ShapeDtypeStruct((512, 896), BF16),
            jax.ShapeDtypeStruct((512, 896), BF16),
            jax.ShapeDtypeStruct((32, 896), BF16),
        ],
        in_specs=[VMEM] * 4,
        out_specs=[ANY] * 3,
        scratch_shapes=[pltpu.VMEM((512, 896), BF16), DMA((6,))],
        compiler_params=pltpu.CompilerParams(vmem_limit_bytes=LIMIT),
    )(ortho, basis, momentum, weight)


def local(weight, gradient, momentum, basis):
    outputs = out_call(*main_call(basis.T, momentum, gradient, weight))
    return outputs[0], outputs[1], outputs[2].T


def solution(mesh):
    return jax.shard_map(
        local,
        mesh=mesh,
        in_specs=(P("row", "col"), P("row", "col"), P("row", "col"), P("col", "row")),
        out_specs=(P("row", "col"), P("row", "col"), P("col", "row")),
        check_vma=False,
    )
```

```python
import math

import jax
import jax.numpy as jnp
from jax import lax
from jax.experimental import pallas as pl
from jax.experimental.pallas import tpu as pltpu
from jax.sharding import PartitionSpec as P

D = 8192
FF = 28672
RANK = 512
ROWS = 16
COLS = 32
TILES = 5
LIMIT = 53 * 2**20
F32 = jnp.float32
BF16 = jnp.bfloat16
MESH = pl.DeviceIdType.MESH
VMEM = pl.BlockSpec(memory_space=pltpu.VMEM)
ANY = pl.BlockSpec(memory_space=pl.ANY)
DMA = pltpu.SemaphoreType.DMA
NN = (((1,), (0,)), ((), ()))
NT = (((1,), (1,)), ((), ()))
TN = (((0,), (0,)), ((), ()))


def remote(src, dst, send, recv, **where):
    return pltpu.make_async_remote_copy(
        src_ref=src, dst_ref=dst, send_sem=send, recv_sem=recv, device_id=where, device_id_type=MESH)


def wait_bytes(ref, sem):
    pltpu.make_async_copy(ref, ref, sem).wait()


def ring(a):
    return lax.rem(a + 2 * ROWS, ROWS)


def greet(r, c):
    barrier = pltpu.get_barrier_semaphore()
    for k in (1, 2, ROWS - 1, ROWS - 2):
        pl.semaphore_signal(barrier, inc=1, device_id={"row": ring(r + k)}, device_id_type=MESH)

    def one(k, carry):
        pl.semaphore_signal(barrier, inc=1, device_id={"col": lax.rem(c + k, COLS)}, device_id_type=MESH)
        return carry

    lax.fori_loop(1, COLS, one, 0)
    return barrier, 4 + COLS - 1


def col_send(c, src_of, dst, send, recv):
    def one(k, carry):
        d = lax.rem(c + 1 + lax.rem(k + COLS // 2 - 1, COLS - 1), COLS)
        remote(src_of(d), dst, send, recv, col=d).start()
        return carry

    lax.fori_loop(0, COLS - 1, one, 0)


class Gather:
    def __init__(self, r, buf, send, recv):
        self.r, self.buf, self.send, self.recv = r, buf, send, recv

    def message(self, way, d, h):
        sign = 1 if way == 0 else -1
        step = 2 - d % 2
        block = self.buf.at[ring(self.r - sign * (d - step)), pl.ds(16 * h, 16), :]
        return remote(block, block, self.send.at[way, d, h], self.recv.at[way, d, h], row=ring(self.r + sign * step))

    def start(self):
        for d in (2, 1):
            for h in range(2):
                for way in range(2):
                    self.message(way, d, h).start()

    def forward(self, d):
        for h in range(2):
            for way in range(2):
                self.message(way, d, h).wait_recv()
                if d + 2 <= 8 - way:
                    self.message(way, d + 2, h).start()
                self.message(way, d + 1, h).start()

    def end(self, d):
        for h in range(2):
            for way in range(2):
                if d <= 8 - way:
                    self.message(way, d, h).wait_recv()

    def drain(self):
        for d in range(1, 9):
            for h in range(2):
                for way in range(2):
                    if d <= 8 - way:
                        self.message(way, d, h).wait_send()


class Reduce:
    def __init__(self, r, part, slots, first, send, recv):
        self.r, self.part, self.slots, self.first, self.send, self.recv = r, part, slots, first, send, recv
        self.size = RANK // ROWS

    def own(self, way, d, h):
        block = ring(self.r + (d if way == 0 else -d))
        return self.part[pl.ds(pl.multiple_of(block * self.size + 16 * h, 16), 16), :]

    def slot(self, way, d, h):
        return self.slots.at[way, d, pl.ds(16 * h, 16), :]

    def message(self, way, d, h, src=None):
        sign = 1 if way == 0 else -1
        slot = self.slot(way, d, h)
        return remote(
            slot if src is None else src, slot, self.send.at[way, d, h], self.recv.at[way, d, h],
            row=ring(self.r + sign * (2 - d % 2)))

    def give(self, way, d, h):
        here = self.first.at[way, d // 2, pl.ds(16 * h, 16), :]
        here[...] = self.own(way, d, h).astype(BF16)
        self.message(way, d, h, here).start()

    def start(self):
        for h in range(2):
            self.give(0, 8, h)
            self.give(1, 7, h)
            self.give(0, 7, h)

    def forward(self, d):
        for h in range(2):
            for way in range(2):
                total = self.own(way, d, h)
                for far in (d + 1, d + 2):
                    if far <= 8 - way:
                        self.message(way, far, h).wait_recv()
                        total = total + self.slot(way, far, h)[...].astype(F32)
                here = self.slot(way, d + 1, h)
                here[...] = total.astype(BF16)
                self.message(way, d, h, here).start()
                self.give(way, d - 1, h)

    def end(self, h):
        total = self.own(0, 0, h)
        for way in range(2):
            for d in (1, 2):
                self.message(way, d, h).wait_recv()
                total = total + self.slot(way, d, h)[...].astype(F32)
        return total

    def drain(self):
        for d in range(1, 9):
            for h in range(2):
                for way in range(2):
                    if d <= 8 - way:
                        self.message(way, d, h).wait_send()


def split(x):
    high = x.astype(BF16)
    return high, (x - high.astype(F32)).astype(BF16)


def parts(x):
    high = x.astype(BF16)
    rest = x - high.astype(F32)
    mid = rest.astype(BF16)
    low = (rest - mid.astype(F32)).astype(BF16)
    return (high, high, mid, high, low, mid), (high, mid, high, low, high, mid)


def dot_exact(a, b):
    return lax.dot_general(
        jnp.concatenate(parts(a)[0], axis=0), jnp.concatenate(parts(b)[1], axis=0), TN, preferred_element_type=F32)


def factor_block(w, spare, midway):
    sub = lax.broadcasted_iota(jnp.int32, (8, 256), 0)
    near = 3

    def twice(x):
        return jnp.concatenate([x, x], axis=1)

    def column(x, k):
        return jnp.broadcast_to(x[:, k:k + 1], (8, 128))

    for p in range(16):
        if p == 8:
            midway()
        panel = w[p]
        rows = [jnp.broadcast_to(w[p, k:k + 1, :], (8, 256)) for k in range(8)]
        s, u, root = {}, {}, {}
        for j in range(8):
            spare[p % 2, j] = column(panel, 8 * p + j)
            for i in range(j + 1):
                s[i, j] = jnp.broadcast_to(spare[p % 2, j, i:i + 1, :], (8, 128))
        for j in range(8):
            root[j] = lax.rsqrt(s[j, j])
            for i in range(j + 1, 8):
                u[j, i] = s[j, i] * root[j]
            for i in range(j + 1, 8):
                for l in range(i, 8):
                    s[i, l] = s[i, l] - u[j, i] * u[j, l]
        for j in range(8):
            rows[j] = rows[j] * twice(root[j])
            for i in range(j + 1, 8):
                rows[i] = rows[i] - twice(u[j, i]) * rows[j]
        for g in range(p + 1, min(16, p + 1 + near)):
            rest = w[g]
            x = [column(rest, 8 * p + k) for k in range(8)]
            for k in range(8):
                x[k] = x[k] * root[k]
                for l in range(k + 1, 8):
                    x[l] = x[l] - x[k] * u[k, l]
            taken = twice(x[0]) * rows[0]
            for k in range(1, 8):
                taken = taken + twice(x[k]) * rows[k]
            w[g] = rest - taken
        done = rows[7]
        for k in range(7):
            done = jnp.where(sub == k, rows[k], done)
        w[p] = done
        far = p + 1 + near
        if far < 16:
            taken = dot_exact(done[:, :128], done)
            w[far:] = w[far:] - taken.reshape(16, 8, 256)[far:]


def factor_rows(work, block, spare, b, midway):
    rows = pl.ds(pl.multiple_of(128 * b, 128), 128)
    live = pl.ds(pl.multiple_of(128 * (b + 1), 128), 512)
    block[:, :, :128] = work[rows, rows].reshape(16, 8, 128)
    block[:, :, 128:] = unit(128).reshape(16, 8, 128)
    factor_block(block, spare, midway)
    inverse = block[:, :, 128:].reshape(128, 128)
    panel = lax.dot_general(
        jnp.concatenate(parts(inverse)[0], axis=1), jnp.concatenate(parts(work[rows, live])[1], axis=0), NN,
        preferred_element_type=F32)
    work[rows, live] = panel

    @pl.when(b < 3)
    def _():
        below = pl.ds(pl.multiple_of(128 * (b + 1), 128), 384)
        work[below, live] = work[below, live] - dot_exact(panel[:, :384], panel)


def unit(rows):
    return jnp.where(
        lax.broadcasted_iota(jnp.int32, (rows, rows), 0) == lax.broadcasted_iota(jnp.int32, (rows, rows), 1), 1.0, 0.0)


def main_kernel(
    basis_in, momentum, gradient, weight, ortho_out, basis_out, momentum_out, weight_out,
    basis_all, loaded, buffer, partial, arrived, lefts, left, order, cross_part, slots, first, cross_all,
    gram_part, gram_send, gram_recv, gram_tiles, gram_all, work, block, spare, sums,
    load_sems, basis_send, basis_recv, red_send, red_recv, cross_send, cross_recv, left_sems, sems,
):
    r, c = lax.axis_index("row"), lax.axis_index("col")
    core = lax.rem(c, 2)
    barrier, count = greet(r, c)
    loads = [
        pltpu.make_async_copy(basis_in, basis_all.at[r], load_sems.at[0]),
        pltpu.make_async_copy(momentum, loaded.at[0], load_sems.at[1]),
        pltpu.make_async_copy(gradient, loaded.at[1], load_sems.at[2]),
    ]
    for load in loads:
        load.start()
    keep = pltpu.make_async_copy(weight, weight_out, load_sems.at[3])
    keep.start()
    work[...] = jnp.zeros((896, 1024), F32)
    for b in range(4):
        work[128 * b:128 * b + 128, 512 + 128 * b:512 + 128 * b + 128] = unit(128)
    position = lax.broadcasted_iota(jnp.int32, (512, 512), 0)
    turn = position >> 5
    far = (turn + 1) >> 1
    natural = (jnp.where((turn & 1) == 1, r - far, r + far) & (ROWS - 1)) * 32 + (position & 31)
    order[...] = jnp.where(natural == lax.broadcasted_iota(jnp.int32, (512, 512), 1), 1.0, 0.0).astype(BF16)
    for load in loads:
        load.wait()
    buffer[...] = (loaded[0].astype(F32) + loaded[1].astype(F32)).astype(BF16)
    pl.semaphore_wait(barrier, count)

    gather = Gather(r, basis_all, basis_send, basis_recv)
    gather.start()

    def blocks(w):
        return [ring(r - (m + 1) // 2 if m % 2 else r + m // 2) for m in range(4 * w, 4 * w + 4)]

    def send_partial(w):
        if w < 3:
            gather.forward(2 * w + 2)
            gather.end(2 * w + 1)
        else:
            gather.end(7)
            gather.end(8)
        columns = jnp.concatenate([basis_all[i] for i in blocks(w)], axis=0)
        partial[w] = lax.dot_general(buffer[...], columns, NT, preferred_element_type=F32).astype(BF16)

        def rows_of(d):
            return partial.at[w, pl.ds(pl.multiple_of(d * 16, 16), 16), :]

        col_send(c, rows_of, arrived.at[w, c], left_sems.at[0, w], left_sems.at[1, w])
        arrived[w, c] = rows_of(c)[...]

    def send_left(w):
        wait_bytes(arrived.at[w, pl.ds(0, COLS - 1)], left_sems.at[1, w])
        total = arrived[w, 0].astype(F32)
        for k in range(1, COLS):
            total = total + arrived[w, k].astype(F32)
        lefts[w, c] = total.astype(BF16)
        col_send(c, lambda d: lefts.at[w, c], lefts.at[w, c], left_sems.at[2, w], left_sems.at[3, w])

    reduce = Reduce(r, cross_part, slots, first, red_send, red_recv)

    def add_cross(w):
        wait_bytes(arrived.at[w, pl.ds(0, COLS - 1)], left_sems.at[3, w])
        part = lax.dot_general(lefts[w].reshape(512, 128), buffer[...], TN, preferred_element_type=F32)
        for i, b in enumerate(blocks(w)):
            cross_part[pl.ds(pl.multiple_of(32 * ring(b + 8), 32), 32), :] = part[32 * i:32 * i + 32, :]

    send_partial(0)
    send_partial(1)
    send_left(0)
    send_partial(2)
    send_left(1)
    add_cross(0)
    reduce.start()
    send_partial(3)
    send_left(2)
    add_cross(1)
    reduce.forward(6)
    send_left(3)
    add_cross(2)
    reduce.forward(4)
    add_cross(3)
    mixed = jnp.concatenate([lefts[w].reshape(512, 128) for w in range(4)], axis=1)
    left[...] = jnp.dot(mixed, order[...], preferred_element_type=F32).astype(BF16)

    quarter = c // 16
    for i in range(2):
        start = quarter if i == 0 else 3 - quarter
        lanes = left[:, pl.ds(pl.multiple_of(start * 128, 128), 128)]
        gram_part[i] = lax.dot_general(lanes, left[...], TN, preferred_element_type=F32)
    low = lax.rem(c, 16)
    for t in range(TILES):
        upper = t < 4 - quarter
        part = jnp.where(upper, 0, 1)
        row = jnp.where(upper, low, 15 - low)
        lane = jnp.where(upper, t + quarter, t - 1)
        gram_send[t] = gram_part[part, pl.ds(pl.multiple_of(row * 8, 8), 8), pl.ds(pl.multiple_of(lane * 128, 128), 128)]

    mine = lax.rem(r, 8)
    reducer = mine < TILES

    def send_tile(k, carry):
        d = ring(r + k)
        t = lax.rem(d, 8)

        @pl.when(t < TILES)
        def _():
            remote(gram_send.at[t], gram_recv.at[r], sems.at[0], sems.at[1], row=d).start()

        return carry

    lax.fori_loop(1, ROWS, send_tile, 0)

    reduce.forward(2)

    @pl.when(reducer)
    def _():
        wait_bytes(gram_recv.at[pl.ds(0, ROWS - 1)], sems.at[1])
        gram_recv[r] = gram_send[mine]
        tile = gram_recv[0]
        for k in range(1, ROWS):
            tile = tile + gram_recv[k]
        gram_tiles[mine] = tile
        for k in (-3, -2, -1, 1, 2, 3, 4):
            remote(gram_tiles.at[mine], gram_tiles.at[mine], sems.at[2], sems.at[3], row=ring(r + k)).start()

    for h in range(2):
        cross_all[r, pl.ds(16 * h, 16), :] = reduce.end(h).astype(BF16)
    spread = Gather(r, cross_all, cross_send, cross_recv)
    spread.start()

    @pl.when(reducer)
    def _():
        wait_bytes(gram_recv.at[pl.ds(0, TILES - 1)], sems.at[3])

    @pl.when(jnp.logical_not(reducer))
    def _():
        wait_bytes(gram_recv.at[pl.ds(0, TILES)], sems.at[3])

    chip = c // 2
    gram_all[core, chip] = gram_tiles[...]

    def send_gram(k, carry):
        remote(gram_all.at[core, chip], gram_all.at[core, chip], sems.at[4], sems.at[5],
               col=lax.rem(c + 2 * k, COLS)).start()
        return carry

    lax.fori_loop(1, COLS // 2, send_gram, 0)
    spread.forward(2)
    wait_bytes(gram_all.at[0, pl.ds(0, 15)], sems.at[5])
    sibling = remote(gram_all.at[core], gram_all.at[core], sems.at[6], sems.at[7], col=c + 1 - 2 * core)
    sibling.start()
    spread.forward(4)
    sibling.wait_recv()

    def place_tiles(k, carry):
        kc = 2 * (k // 2) + lax.rem(k, 2)
        kq = kc // 16
        for t in range(TILES):
            upper = t < 4 - kq
            row = jnp.where(upper, kc, 63 - kc)
            lane = jnp.where(upper, t + kq, t - 1)
            work[pl.ds(pl.multiple_of(row * 8, 8), 8), pl.ds(pl.multiple_of(lane * 128, 128), 128)] = (
                gram_all[lax.rem(k, 2), k // 2, t])
        return carry

    lax.fori_loop(0, COLS, place_tiles, 0)
    def factor_step(b, carry):
        def midway():
            @pl.when(b == 0)
            def _():
                spread.forward(6)

        factor_rows(work, block, spare, b, midway)
        return carry

    lax.fori_loop(0, 4, factor_step, 0)
    for d in (1, 3, 5, 7, 8):
        spread.end(d)

    high, low_part = split(work[:512, 512:])
    cross = jnp.concatenate([cross_all[8:], cross_all[:8]], axis=0).reshape(512, 896)
    right = jnp.dot(high, cross, preferred_element_type=F32) + jnp.dot(low_part, cross, preferred_element_type=F32)
    square_high, square_low = split(right * right)
    ones = jnp.ones((8, 896), BF16)
    total = (
        lax.dot_general(ones, square_high, NT, preferred_element_type=F32)
        + lax.dot_general(ones, square_low, NT, preferred_element_type=F32))
    sub = lax.broadcasted_iota(jnp.int32, (8, 128), 0)
    tile = total[:, :128]
    for q in range(1, 4):
        tile = jnp.where(sub == q, total[:, 128 * q:128 * q + 128], tile)
    sums[c] = tile
    col_send(c, lambda d: sums.at[c], sums.at[c], sems.at[8], sems.at[9])
    ortho = (
        lax.dot_general(left[...], high, NT, preferred_element_type=F32)
        + lax.dot_general(left[...], low_part, NT, preferred_element_type=F32)).astype(BF16)
    ortho_out[...] = ortho
    correction = jnp.dot(ortho, right.astype(BF16), preferred_element_type=F32)
    momentum_out[...] = (buffer[...].astype(F32) - 0.2 * correction).astype(BF16)
    keep.wait()

    gather.drain()
    reduce.drain()
    spread.drain()
    for w in range(4):
        wait_bytes(arrived.at[w, pl.ds(0, COLS - 1)], left_sems.at[0, w])
        wait_bytes(arrived.at[w, pl.ds(0, COLS - 1)], left_sems.at[2, w])

    @pl.when(reducer)
    def _():
        wait_bytes(gram_recv.at[pl.ds(0, 2 * TILES - 1)], sems.at[0])
        wait_bytes(gram_recv.at[pl.ds(0, 7)], sems.at[2])

    @pl.when(jnp.logical_not(reducer))
    def _():
        wait_bytes(gram_recv.at[pl.ds(0, 2 * TILES)], sems.at[0])

    wait_bytes(gram_all.at[0, pl.ds(0, 15)], sems.at[4])
    sibling.wait_send()
    wait_bytes(sums.at[pl.ds(0, COLS - 1)], sems.at[8])
    wait_bytes(sums.at[pl.ds(0, COLS - 1)], sems.at[9])
    total = sums[0]
    for k in range(1, COLS):
        total = total + sums[k]
    scale = lax.rsqrt(total / FF + 1e-06).T
    for q in range(4):
        basis_out[128 * q:128 * q + 128, :] = (right[128 * q:128 * q + 128, :] * scale[:, q:q + 1]).astype(BF16)


def main_call(basis_t, momentum, gradient, weight):
    return pl.pallas_call(
        main_kernel,
        out_shape=[
            jax.ShapeDtypeStruct((512, 512), BF16),
            jax.ShapeDtypeStruct((512, 896), BF16),
            jax.ShapeDtypeStruct((512, 896), BF16),
            jax.ShapeDtypeStruct((512, 896), BF16),
        ],
        in_specs=[ANY] * 4,
        out_specs=[VMEM] * 4,
        scratch_shapes=[
            pltpu.VMEM((ROWS, 32, 896), BF16),
            pltpu.VMEM((2, 512, 896), BF16),
            pltpu.VMEM((512, 896), BF16),
            pltpu.VMEM((4, 512, 128), BF16),
            pltpu.VMEM((4, COLS, 16, 128), BF16),
            pltpu.VMEM((4, COLS, 16, 128), BF16),
            pltpu.VMEM((512, 512), BF16),
            pltpu.VMEM((512, 512), BF16),
            pltpu.VMEM((512, 896), F32),
            pltpu.VMEM((2, 9, 32, 896), BF16),
            pltpu.VMEM((2, 5, 32, 896), BF16),
            pltpu.VMEM((ROWS, 32, 896), BF16),
            pltpu.VMEM((2, 128, 512), F32),
            pltpu.VMEM((TILES, 8, 128), F32),
            pltpu.VMEM((ROWS, 8, 128), F32),
            pltpu.VMEM((TILES, 8, 128), F32),
            pltpu.VMEM((2, COLS // 2, TILES, 8, 128), F32),
            pltpu.VMEM((896, 1024), F32),
            pltpu.VMEM((16, 8, 256), F32),
            pltpu.VMEM((2, 8, 8, 128), F32),
            pltpu.VMEM((COLS, 8, 128), F32),
            DMA((4,)),
            DMA((2, 9, 2)), DMA((2, 9, 2)),
            DMA((2, 9, 2)), DMA((2, 9, 2)),
            DMA((2, 9, 2)), DMA((2, 9, 2)),
            DMA((4, 4)),
            DMA((10,)),
        ],
        compiler_params=pltpu.CompilerParams(
            collective_id=0, has_side_effects=True, vmem_limit_bytes=LIMIT),
    )(basis_t, momentum, gradient, weight)


def out_kernel(ortho, basis, momentum, weight, new_weight, new_momentum, new_basis_t, done, sems):
    r = lax.axis_index("row")
    copies = [
        pltpu.make_async_copy(momentum, new_momentum, sems.at[0]),
        pltpu.make_async_copy(basis.at[pl.ds(pl.multiple_of(r * 32, 32), 32), :], new_basis_t, sems.at[1]),
    ]
    for copy in copies:
        copy.start()
    for q in range(4):
        rows = pl.ds(128 * q, 128)
        update = jnp.dot(ortho[rows, :], basis[...], preferred_element_type=F32)
        done[rows, :] = (weight[rows, :].astype(F32) - 0.5 * math.sqrt(D / RANK) * update).astype(BF16)
        copies.append(pltpu.make_async_copy(done.at[rows, :], new_weight.at[rows, :], sems.at[2 + q]))
        copies[2 + q].start()
    for copy in copies:
        copy.wait()


def out_call(ortho, basis, momentum, weight):
    return pl.pallas_call(
        out_kernel,
        out_shape=[
            jax.ShapeDtypeStruct((512, 896), BF16),
            jax.ShapeDtypeStruct((512, 896), BF16),
            jax.ShapeDtypeStruct((32, 896), BF16),
        ],
        in_specs=[VMEM] * 4,
        out_specs=[ANY] * 3,
        scratch_shapes=[pltpu.VMEM((512, 896), BF16), DMA((6,))],
        compiler_params=pltpu.CompilerParams(vmem_limit_bytes=LIMIT),
    )(ortho, basis, momentum, weight)


def local(weight, gradient, momentum, basis):
    outputs = out_call(*main_call(basis.T, momentum, gradient, weight))
    return outputs[0], outputs[1], outputs[2].T


def solution(mesh):
    return jax.shard_map(
        local,
        mesh=mesh,
        in_specs=(P("row", "col"), P("row", "col"), P("row", "col"), P("col", "row")),
        out_specs=(P("row", "col"), P("row", "col"), P("col", "row")),
        check_vma=False,
    )
```

```python
import math

import jax
import jax.numpy as jnp
from jax import lax
from jax.experimental import pallas as pl
from jax.experimental.pallas import tpu as pltpu
from jax.sharding import PartitionSpec as P

D = 8192
FF = 28672
RANK = 512
ROWS = 16
COLS = 32
TILES = 5
LIMIT = 50 * 2**20
F32 = jnp.float32
BF16 = jnp.bfloat16
MESH = pl.DeviceIdType.MESH
VMEM = pl.BlockSpec(memory_space=pltpu.VMEM)
ANY = pl.BlockSpec(memory_space=pl.ANY)
DMA = pltpu.SemaphoreType.DMA
NN = (((1,), (0,)), ((), ()))
NT = (((1,), (1,)), ((), ()))
TN = (((0,), (0,)), ((), ()))


def remote(src, dst, send, recv, **where):
    return pltpu.make_async_remote_copy(
        src_ref=src, dst_ref=dst, send_sem=send, recv_sem=recv, device_id=where, device_id_type=MESH)


def wait_bytes(ref, sem):
    pltpu.make_async_copy(ref, ref, sem).wait()


def ring(a):
    return lax.rem(a + 2 * ROWS, ROWS)


def greet(r, c):
    barrier = pltpu.get_barrier_semaphore()
    for k in (1, 2, ROWS - 1, ROWS - 2):
        pl.semaphore_signal(barrier, inc=1, device_id={"row": ring(r + k)}, device_id_type=MESH)

    def one(k, carry):
        pl.semaphore_signal(barrier, inc=1, device_id={"col": lax.rem(c + k, COLS)}, device_id_type=MESH)
        return carry

    lax.fori_loop(1, COLS, one, 0)
    return barrier, 4 + COLS - 1


def col_send(c, src_of, dst, send, recv):
    def one(k, carry):
        d = lax.rem(c + 1 + lax.rem(k + COLS // 2 - 1, COLS - 1), COLS)
        remote(src_of(d), dst, send, recv, col=d).start()
        return carry

    lax.fori_loop(0, COLS - 1, one, 0)


class Gather:
    def __init__(self, r, buf, send, recv):
        self.r, self.buf, self.send, self.recv = r, buf, send, recv

    def message(self, way, d, h):
        sign = 1 if way == 0 else -1
        step = 2 - d % 2
        block = self.buf.at[ring(self.r - sign * (d - step)), pl.ds(16 * h, 16), :]
        return remote(block, block, self.send.at[way, d, h], self.recv.at[way, d, h], row=ring(self.r + sign * step))

    def start(self):
        for d in (2, 1):
            for h in range(2):
                for way in range(2):
                    self.message(way, d, h).start()

    def forward(self, d):
        for h in range(2):
            for way in range(2):
                self.message(way, d, h).wait_recv()
                if d + 2 <= 8 - way:
                    self.message(way, d + 2, h).start()
                self.message(way, d + 1, h).start()

    def end(self, d):
        for h in range(2):
            for way in range(2):
                if d <= 8 - way:
                    self.message(way, d, h).wait_recv()

    def drain(self):
        for d in range(1, 9):
            for h in range(2):
                for way in range(2):
                    if d <= 8 - way:
                        self.message(way, d, h).wait_send()


class Reduce:
    def __init__(self, r, part, slots, first, send, recv):
        self.r, self.part, self.slots, self.first, self.send, self.recv = r, part, slots, first, send, recv
        self.size = RANK // ROWS

    def own(self, way, d, h):
        block = ring(self.r + (d if way == 0 else -d))
        return self.part[pl.ds(pl.multiple_of(block * self.size + 16 * h, 16), 16), :]

    def slot(self, way, d, h):
        return self.slots.at[way, d, pl.ds(16 * h, 16), :]

    def message(self, way, d, h, src=None):
        sign = 1 if way == 0 else -1
        slot = self.slot(way, d, h)
        return remote(
            slot if src is None else src, slot, self.send.at[way, d, h], self.recv.at[way, d, h],
            row=ring(self.r + sign * (2 - d % 2)))

    def give(self, way, d, h):
        here = self.first.at[way, d // 2, pl.ds(16 * h, 16), :]
        here[...] = self.own(way, d, h).astype(BF16)
        self.message(way, d, h, here).start()

    def start(self):
        for h in range(2):
            self.give(0, 8, h)
            self.give(1, 7, h)
            self.give(0, 7, h)

    def forward(self, d):
        for h in range(2):
            for way in range(2):
                total = self.own(way, d, h)
                for far in (d + 1, d + 2):
                    if far <= 8 - way:
                        self.message(way, far, h).wait_recv()
                        total = total + self.slot(way, far, h)[...].astype(F32)
                here = self.slot(way, d + 1, h)
                here[...] = total.astype(BF16)
                self.message(way, d, h, here).start()
                self.give(way, d - 1, h)

    def end(self, h):
        total = self.own(0, 0, h)
        for way in range(2):
            for d in (1, 2):
                self.message(way, d, h).wait_recv()
                total = total + self.slot(way, d, h)[...].astype(F32)
        return total

    def drain(self):
        for d in range(1, 9):
            for h in range(2):
                for way in range(2):
                    if d <= 8 - way:
                        self.message(way, d, h).wait_send()


def split(x):
    high = x.astype(BF16)
    return high, (x - high.astype(F32)).astype(BF16)


def parts(x):
    high = x.astype(BF16)
    rest = x - high.astype(F32)
    mid = rest.astype(BF16)
    low = (rest - mid.astype(F32)).astype(BF16)
    return (high, high, mid, high, low, mid), (high, mid, high, low, high, mid)


def dot_exact(a, b):
    return lax.dot_general(
        jnp.concatenate(parts(a)[0], axis=0), jnp.concatenate(parts(b)[1], axis=0), TN, preferred_element_type=F32)


def factor_block(w, spare, midway):
    sub = lax.broadcasted_iota(jnp.int32, (8, 256), 0)
    near = 3

    def twice(x):
        return jnp.concatenate([x, x], axis=1)

    def column(x, k):
        return jnp.broadcast_to(x[:, k:k + 1], (8, 128))

    for p in range(16):
        if p == 8:
            midway()
        panel = w[p]
        rows = [jnp.broadcast_to(w[p, k:k + 1, :], (8, 256)) for k in range(8)]
        s, u, root = {}, {}, {}
        for j in range(8):
            spare[p % 2, j] = column(panel, 8 * p + j)
            for i in range(j + 1):
                s[i, j] = jnp.broadcast_to(spare[p % 2, j, i:i + 1, :], (8, 128))
        for j in range(8):
            root[j] = lax.rsqrt(s[j, j])
            for i in range(j + 1, 8):
                u[j, i] = s[j, i] * root[j]
            for i in range(j + 1, 8):
                for l in range(i, 8):
                    s[i, l] = s[i, l] - u[j, i] * u[j, l]
        for j in range(8):
            rows[j] = rows[j] * twice(root[j])
            for i in range(j + 1, 8):
                rows[i] = rows[i] - twice(u[j, i]) * rows[j]
        for g in range(p + 1, min(16, p + 1 + near)):
            rest = w[g]
            x = [column(rest, 8 * p + k) for k in range(8)]
            for k in range(8):
                x[k] = x[k] * root[k]
                for l in range(k + 1, 8):
                    x[l] = x[l] - x[k] * u[k, l]
            taken = twice(x[0]) * rows[0]
            for k in range(1, 8):
                taken = taken + twice(x[k]) * rows[k]
            w[g] = rest - taken
        done = rows[7]
        for k in range(7):
            done = jnp.where(sub == k, rows[k], done)
        w[p] = done
        far = p + 1 + near
        if far < 16:
            taken = dot_exact(done[:, :128], done)
            w[far:] = w[far:] - taken.reshape(16, 8, 256)[far:]


def factor_rows(work, block, spare, b, midway):
    rows = pl.ds(pl.multiple_of(128 * b, 128), 128)
    live = pl.ds(pl.multiple_of(128 * (b + 1), 128), 512)
    block[:, :, :128] = work[rows, rows].reshape(16, 8, 128)
    block[:, :, 128:] = unit(128).reshape(16, 8, 128)
    factor_block(block, spare, midway)
    inverse = block[:, :, 128:].reshape(128, 128)
    panel = lax.dot_general(
        jnp.concatenate(parts(inverse)[0], axis=1), jnp.concatenate(parts(work[rows, live])[1], axis=0), NN,
        preferred_element_type=F32)
    work[rows, live] = panel

    @pl.when(b < 3)
    def _():
        below = pl.ds(pl.multiple_of(128 * (b + 1), 128), 384)
        work[below, live] = work[below, live] - dot_exact(panel[:, :384], panel)


def unit(rows):
    return jnp.where(
        lax.broadcasted_iota(jnp.int32, (rows, rows), 0) == lax.broadcasted_iota(jnp.int32, (rows, rows), 1), 1.0, 0.0)


def main_kernel(
    basis_in, momentum, gradient, weight, ortho_out, basis_out, momentum_out, weight_out,
    basis_all, loaded, buffer, partial, arrived, lefts, left, order, cross_part, slots, first, cross_all,
    gram_part, gram_send, gram_recv, gram_tiles, gram_all, work, block, spare, sums,
    load_sems, basis_send, basis_recv, red_send, red_recv, cross_send, cross_recv, left_sems, sems,
):
    r, c = lax.axis_index("row"), lax.axis_index("col")
    core = lax.rem(c, 2)
    barrier, count = greet(r, c)
    loads = [
        pltpu.make_async_copy(basis_in, basis_all.at[r], load_sems.at[0]),
        pltpu.make_async_copy(momentum, loaded.at[0], load_sems.at[1]),
        pltpu.make_async_copy(gradient, loaded.at[1], load_sems.at[2]),
    ]
    for load in loads:
        load.start()
    keep = pltpu.make_async_copy(weight, weight_out, load_sems.at[3])
    keep.start()
    work[...] = jnp.zeros((896, 1024), F32)
    for b in range(4):
        work[128 * b:128 * b + 128, 512 + 128 * b:512 + 128 * b + 128] = unit(128)
    position = lax.broadcasted_iota(jnp.int32, (512, 512), 0)
    turn = position >> 5
    far = (turn + 1) >> 1
    natural = (jnp.where((turn & 1) == 1, r - far, r + far) & (ROWS - 1)) * 32 + (position & 31)
    order[...] = jnp.where(natural == lax.broadcasted_iota(jnp.int32, (512, 512), 1), 1.0, 0.0).astype(BF16)
    for load in loads:
        load.wait()
    buffer[...] = (loaded[0].astype(F32) + loaded[1].astype(F32)).astype(BF16)
    pl.semaphore_wait(barrier, count)

    gather = Gather(r, basis_all, basis_send, basis_recv)
    gather.start()

    def blocks(w):
        return [ring(r - (m + 1) // 2 if m % 2 else r + m // 2) for m in range(4 * w, 4 * w + 4)]

    def send_partial(w):
        if w < 3:
            gather.forward(2 * w + 2)
            gather.end(2 * w + 1)
        else:
            gather.end(7)
            gather.end(8)
        columns = jnp.concatenate([basis_all[i] for i in blocks(w)], axis=0)
        partial[w] = lax.dot_general(buffer[...], columns, NT, preferred_element_type=F32).astype(BF16)

        def rows_of(d):
            return partial.at[w, pl.ds(pl.multiple_of(d * 16, 16), 16), :]

        col_send(c, rows_of, arrived.at[w, c], left_sems.at[0, w], left_sems.at[1, w])
        arrived[w, c] = rows_of(c)[...]

    def send_left(w):
        wait_bytes(arrived.at[w, pl.ds(0, COLS - 1)], left_sems.at[1, w])
        total = arrived[w, 0].astype(F32)
        for k in range(1, COLS):
            total = total + arrived[w, k].astype(F32)
        lefts[w, c] = total.astype(BF16)
        col_send(c, lambda d: lefts.at[w, c], lefts.at[w, c], left_sems.at[2, w], left_sems.at[3, w])

    reduce = Reduce(r, cross_part, slots, first, red_send, red_recv)

    def add_cross(w):
        wait_bytes(arrived.at[w, pl.ds(0, COLS - 1)], left_sems.at[3, w])
        part = lax.dot_general(lefts[w].reshape(512, 128), buffer[...], TN, preferred_element_type=F32)
        for i, b in enumerate(blocks(w)):
            cross_part[pl.ds(pl.multiple_of(32 * ring(b + 8), 32), 32), :] = part[32 * i:32 * i + 32, :]

    send_partial(0)
    send_partial(1)
    send_left(0)
    send_partial(2)
    send_left(1)
    add_cross(0)
    reduce.start()
    send_partial(3)
    send_left(2)
    add_cross(1)
    reduce.forward(6)
    send_left(3)
    add_cross(2)
    reduce.forward(4)
    add_cross(3)
    mixed = jnp.concatenate([lefts[w].reshape(512, 128) for w in range(4)], axis=1)
    left[...] = jnp.dot(mixed, order[...], preferred_element_type=F32).astype(BF16)

    quarter = c // 16
    for i in range(2):
        start = quarter if i == 0 else 3 - quarter
        lanes = left[:, pl.ds(pl.multiple_of(start * 128, 128), 128)]
        gram_part[i] = lax.dot_general(lanes, left[...], TN, preferred_element_type=F32)
    low = lax.rem(c, 16)
    for t in range(TILES):
        upper = t < 4 - quarter
        part = jnp.where(upper, 0, 1)
        row = jnp.where(upper, low, 15 - low)
        lane = jnp.where(upper, t + quarter, t - 1)
        gram_send[t] = gram_part[part, pl.ds(pl.multiple_of(row * 8, 8), 8), pl.ds(pl.multiple_of(lane * 128, 128), 128)]

    mine = lax.rem(r, 8)
    reducer = mine < TILES

    def send_tile(k, carry):
        d = ring(r + k)
        t = lax.rem(d, 8)

        @pl.when(t < TILES)
        def _():
            remote(gram_send.at[t], gram_recv.at[r], sems.at[0], sems.at[1], row=d).start()

        return carry

    lax.fori_loop(1, ROWS, send_tile, 0)

    reduce.forward(2)

    @pl.when(reducer)
    def _():
        wait_bytes(gram_recv.at[pl.ds(0, ROWS - 1)], sems.at[1])
        gram_recv[r] = gram_send[mine]
        tile = gram_recv[0]
        for k in range(1, ROWS):
            tile = tile + gram_recv[k]
        gram_tiles[mine] = tile
        for k in (-3, -2, -1, 1, 2, 3, 4):
            remote(gram_tiles.at[mine], gram_tiles.at[mine], sems.at[2], sems.at[3], row=ring(r + k)).start()

    for h in range(2):
        cross_all[r, pl.ds(16 * h, 16), :] = reduce.end(h).astype(BF16)
    spread = Gather(r, cross_all, cross_send, cross_recv)
    spread.start()

    @pl.when(reducer)
    def _():
        wait_bytes(gram_recv.at[pl.ds(0, TILES - 1)], sems.at[3])

    @pl.when(jnp.logical_not(reducer))
    def _():
        wait_bytes(gram_recv.at[pl.ds(0, TILES)], sems.at[3])

    chip = c // 2
    gram_all[core, chip] = gram_tiles[...]

    def send_gram(k, carry):
        remote(gram_all.at[core, chip], gram_all.at[core, chip], sems.at[4], sems.at[5],
               col=lax.rem(c + 2 * k, COLS)).start()
        return carry

    lax.fori_loop(1, COLS // 2, send_gram, 0)
    spread.forward(2)
    wait_bytes(gram_all.at[0, pl.ds(0, 15)], sems.at[5])
    sibling = remote(gram_all.at[core], gram_all.at[core], sems.at[6], sems.at[7], col=c + 1 - 2 * core)
    sibling.start()
    spread.forward(4)
    sibling.wait_recv()

    def place_tiles(k, carry):
        kc = 2 * (k // 2) + lax.rem(k, 2)
        kq = kc // 16
        for t in range(TILES):
            upper = t < 4 - kq
            row = jnp.where(upper, kc, 63 - kc)
            lane = jnp.where(upper, t + kq, t - 1)
            work[pl.ds(pl.multiple_of(row * 8, 8), 8), pl.ds(pl.multiple_of(lane * 128, 128), 128)] = (
                gram_all[lax.rem(k, 2), k // 2, t])
        return carry

    lax.fori_loop(0, COLS, place_tiles, 0)
    def factor_step(b, carry):
        def midway():
            @pl.when(b == 0)
            def _():
                spread.forward(6)

        factor_rows(work, block, spare, b, midway)
        return carry

    lax.fori_loop(0, 4, factor_step, 0)
    for d in (1, 3, 5, 7, 8):
        spread.end(d)

    high, low_part = split(work[:512, 512:])
    cross = jnp.concatenate([cross_all[8:], cross_all[:8]], axis=0).reshape(512, 896)
    right = jnp.dot(high, cross, preferred_element_type=F32) + jnp.dot(low_part, cross, preferred_element_type=F32)
    square_high, square_low = split(right * right)
    ones = jnp.ones((8, 896), BF16)
    total = (
        lax.dot_general(ones, square_high, NT, preferred_element_type=F32)
        + lax.dot_general(ones, square_low, NT, preferred_element_type=F32))
    sub = lax.broadcasted_iota(jnp.int32, (8, 128), 0)
    tile = total[:, :128]
    for q in range(1, 4):
        tile = jnp.where(sub == q, total[:, 128 * q:128 * q + 128], tile)
    sums[c] = tile
    col_send(c, lambda d: sums.at[c], sums.at[c], sems.at[8], sems.at[9])
    ortho = (
        lax.dot_general(left[...], high, NT, preferred_element_type=F32)
        + lax.dot_general(left[...], low_part, NT, preferred_element_type=F32)).astype(BF16)
    ortho_out[...] = ortho
    correction = jnp.dot(ortho, right.astype(BF16), preferred_element_type=F32)
    momentum_out[...] = (buffer[...].astype(F32) - 0.2 * correction).astype(BF16)
    keep.wait()

    gather.drain()
    reduce.drain()
    spread.drain()
    for w in range(4):
        wait_bytes(arrived.at[w, pl.ds(0, COLS - 1)], left_sems.at[0, w])
        wait_bytes(arrived.at[w, pl.ds(0, COLS - 1)], left_sems.at[2, w])

    @pl.when(reducer)
    def _():
        wait_bytes(gram_recv.at[pl.ds(0, 2 * TILES - 1)], sems.at[0])
        wait_bytes(gram_recv.at[pl.ds(0, 7)], sems.at[2])

    @pl.when(jnp.logical_not(reducer))
    def _():
        wait_bytes(gram_recv.at[pl.ds(0, 2 * TILES)], sems.at[0])

    wait_bytes(gram_all.at[0, pl.ds(0, 15)], sems.at[4])
    sibling.wait_send()
    wait_bytes(sums.at[pl.ds(0, COLS - 1)], sems.at[8])
    wait_bytes(sums.at[pl.ds(0, COLS - 1)], sems.at[9])
    total = sums[0]
    for k in range(1, COLS):
        total = total + sums[k]
    scale = lax.rsqrt(total / FF + 1e-06).T
    for q in range(4):
        basis_out[128 * q:128 * q + 128, :] = (right[128 * q:128 * q + 128, :] * scale[:, q:q + 1]).astype(BF16)


def main_call(basis_t, momentum, gradient, weight):
    return pl.pallas_call(
        main_kernel,
        out_shape=[
            jax.ShapeDtypeStruct((512, 512), BF16),
            jax.ShapeDtypeStruct((512, 896), BF16),
            jax.ShapeDtypeStruct((512, 896), BF16),
            jax.ShapeDtypeStruct((512, 896), BF16),
        ],
        in_specs=[ANY] * 4,
        out_specs=[VMEM] * 4,
        scratch_shapes=[
            pltpu.VMEM((ROWS, 32, 896), BF16),
            pltpu.VMEM((2, 512, 896), BF16),
            pltpu.VMEM((512, 896), BF16),
            pltpu.VMEM((4, 512, 128), BF16),
            pltpu.VMEM((4, COLS, 16, 128), BF16),
            pltpu.VMEM((4, COLS, 16, 128), BF16),
            pltpu.VMEM((512, 512), BF16),
            pltpu.VMEM((512, 512), BF16),
            pltpu.VMEM((512, 896), F32),
            pltpu.VMEM((2, 9, 32, 896), BF16),
            pltpu.VMEM((2, 5, 32, 896), BF16),
            pltpu.VMEM((ROWS, 32, 896), BF16),
            pltpu.VMEM((2, 128, 512), F32),
            pltpu.VMEM((TILES, 8, 128), F32),
            pltpu.VMEM((ROWS, 8, 128), F32),
            pltpu.VMEM((TILES, 8, 128), F32),
            pltpu.VMEM((2, COLS // 2, TILES, 8, 128), F32),
            pltpu.VMEM((896, 1024), F32),
            pltpu.VMEM((16, 8, 256), F32),
            pltpu.VMEM((2, 8, 8, 128), F32),
            pltpu.VMEM((COLS, 8, 128), F32),
            DMA((4,)),
            DMA((2, 9, 2)), DMA((2, 9, 2)),
            DMA((2, 9, 2)), DMA((2, 9, 2)),
            DMA((2, 9, 2)), DMA((2, 9, 2)),
            DMA((4, 4)),
            DMA((10,)),
        ],
        compiler_params=pltpu.CompilerParams(
            collective_id=0, has_side_effects=True, vmem_limit_bytes=LIMIT),
    )(basis_t, momentum, gradient, weight)


def out_kernel(ortho, basis, momentum, weight, new_weight, new_momentum, new_basis_t, done, sems):
    r = lax.axis_index("row")
    copies = [
        pltpu.make_async_copy(momentum, new_momentum, sems.at[0]),
        pltpu.make_async_copy(basis.at[pl.ds(pl.multiple_of(r * 32, 32), 32), :], new_basis_t, sems.at[1]),
    ]
    for copy in copies:
        copy.start()
    for q in range(4):
        rows = pl.ds(128 * q, 128)
        update = jnp.dot(ortho[rows, :], basis[...], preferred_element_type=F32)
        done[rows, :] = (weight[rows, :].astype(F32) - 0.5 * math.sqrt(D / RANK) * update).astype(BF16)
        copies.append(pltpu.make_async_copy(done.at[rows, :], new_weight.at[rows, :], sems.at[2 + q]))
        copies[2 + q].start()
    for copy in copies:
        copy.wait()


def out_call(ortho, basis, momentum, weight):
    return pl.pallas_call(
        out_kernel,
        out_shape=[
            jax.ShapeDtypeStruct((512, 896), BF16),
            jax.ShapeDtypeStruct((512, 896), BF16),
            jax.ShapeDtypeStruct((32, 896), BF16),
        ],
        in_specs=[VMEM] * 4,
        out_specs=[ANY] * 3,
        scratch_shapes=[pltpu.VMEM((512, 896), BF16), DMA((6,))],
        compiler_params=pltpu.CompilerParams(vmem_limit_bytes=LIMIT),
    )(ortho, basis, momentum, weight)


def local(weight, gradient, momentum, basis):
    outputs = out_call(*main_call(basis.T, momentum, gradient, weight))
    return outputs[0], outputs[1], outputs[2].T


def solution(mesh):
    return jax.shard_map(
        local,
        mesh=mesh,
        in_specs=(P("row", "col"), P("row", "col"), P("row", "col"), P("col", "row")),
        out_specs=(P("row", "col"), P("row", "col"), P("col", "row")),
        check_vma=False,
    )
```
